768 devices in a mesh: dp: 12 (over z), mp: 64 (over y, x, core).
Axes of the slice: x: 4, y: 8, z: 12, core: 2. Of those that a mesh axis runs over, the one named last changes fastest.
Arguments:
- inputs: float32 [1536, 8192], P('dp', 'mp'), may hold values from -6 to 6
- block_weights: float32 [2432, 128, 128], P('mp'), may hold values from -0.21875 to 0.21875
- block_list: int32 [2432, 2], P('mp'), may hold values from -1 to 63, as said below
- grad_act: float32 [1536, 32768], P('dp', 'mp'), may hold values from -6 to 6
Outputs:
- act: float32 [1536, 32768], P('dp', 'mp')
- grad_inputs: float32 [1536, 8192], P('dp', 'mp')
- grad_weights: float32 [2432, 128, 128], P('mp')
The draws below stay inside these ranges and needn't reach their ends.
Inputs may be any that keep to these rules, and one draw needn't show every extreme that they name: `block_list`: rows s * 38 to s * 38 + 37 belong to index s of mp. A live slot holds a row block below 64 and a local column block below 4; the live slots of one index name distinct cells, and come before its empty slots, which hold -1 in both entries. Each index has 12 to 38 live slots; some index has all 38 live.
All inputs are finite; a program needn't handle non-finite values.
Results may differ from the reference program's by a relative error of at most 0.0056.
Values may be sent and summed in bfloat16 or wider, within the bound.
No kernel may reach another device: no remote copies, remote signals or barrier semaphores. Data moves between devices by JAX's collectives and lax.ppermute only.
A program may use at most 32 MiB of HBM per device.

```python
import jax
import jax.numpy as jnp
from jax import lax

BS = 128
D = 8192
H = 32768
DB = 64
CB = 4
BMAX = 38
TOKENS = 1536
N_MP = 64


def draw_block_list(key, part):
    key = jax.random.fold_in(key, 11)
    cells = DB * CB
    keys = jax.random.split(key, N_MP + 2)
    counts = jax.random.randint(keys[0], (N_MP,), BMAX // 3, BMAX + 1)
    full_dev = jax.random.randint(keys[1], (), 0, N_MP)
    counts = jnp.where(jnp.arange(N_MP) == full_dev, BMAX, counts)

    def pick_cells(one_key):
        return jax.random.permutation(one_key, cells)[:BMAX]
    chosen = jax.vmap(pick_cells)(keys[2:])
    live = jnp.arange(BMAX)[None, :] < counts[:, None]
    rows = jnp.where(live, chosen // CB, -1)
    cols = jnp.where(live, chosen % CB, -1)
    return jnp.stack([rows, cols], -1).reshape(N_MP * BMAX, 2).astype(jnp.int32)


def steps_of(stream_key, shape, cuts, smallest, high):
    def one(position, parts):
        heights = jax.random.uniform(jax.random.fold_in(jax.random.fold_in(stream_key, 6), position), (parts,), jnp.float32, smallest / len(cuts), high / len(cuts))
        return jnp.repeat(jnp.exp(heights), shape[position] // parts).reshape((-1,) + (1,) * (len(shape) - position - 1))

    level = one(*cuts[0])
    for cut in cuts[1:]:
        level = level * one(*cut)
    return level


def bell_draw(stream_key, shape, deviation, limit, shards=(), kind=jnp.bfloat16):
    level = steps_of(stream_key, shape, shards, -0.22, 0.18) if shards else 1.0
    values = jax.random.normal(stream_key, shape, jnp.float32) * deviation * level
    return jnp.minimum(jnp.maximum(values, -limit), limit).astype(kind)


def setup_inputs(seed: int = 0) -> dict:
    key_of = jax.random.split(jax.random.key(seed), 5)
    return {
        "inputs": bell_draw(key_of[0], (TOKENS, D), 1.0, 6.0, ((0, 12), (1, 64)), jnp.float32),
        "block_weights": bell_draw(key_of[1], (N_MP * BMAX, BS, BS), (DB * BS // 10) ** -0.5, 0.21875, ((0, 64),), jnp.float32),
        "block_list": draw_block_list(jax.random.fold_in(key_of[4], 71), 0),
        "grad_act": bell_draw(key_of[3], (TOKENS, H), 1.0, 6.0, ((0, 12), (1, 64)), jnp.float32),
    }


def gelu_parts(pre):
    inner = 0.7978845608 * (pre + 0.044715 * pre * pre * pre)
    tanh_val = jnp.tanh(inner)
    value = 0.5 * pre * (1.0 + tanh_val)
    slope = 0.5 * (1.0 + tanh_val) + 0.5 * pre * (1.0 - tanh_val * tanh_val) * 0.7978845608 * (1.0 + 3.0 * 0.044715 * pre * pre)
    return value, slope


def reference(inputs, block_weights, block_list, grad_act):
    slots = block_list.shape[0]
    per_dev = slots // N_MP
    col_dev = H // N_MP // BS
    xb = inputs.astype(jnp.bfloat16)
    wb = block_weights.astype(jnp.bfloat16)
    row_ids = block_list[:, 0]
    col_ids = block_list[:, 1]
    livef = (row_ids >= 0).astype(jnp.float32)
    owner = (jnp.arange(slots, dtype=jnp.int32) // per_dev).astype(jnp.int32)
    grow = jnp.maximum(row_ids, 0).astype(jnp.int32)
    gcol = (owner * col_dev + jnp.maximum(col_ids, 0)).astype(jnp.int32)

    def forward(pre, item):
        row_one, col_one, live_one, weight = item
        xs = lax.dynamic_slice_in_dim(xb, (row_one * BS).astype(jnp.int32), BS, 1)
        part = jnp.dot(xs, weight, preferred_element_type=jnp.float32) * live_one
        start = (col_one * BS).astype(jnp.int32)
        current = lax.dynamic_slice_in_dim(pre, start, BS, 1)
        return lax.dynamic_update_slice_in_dim(pre, current + part, start, 1), None

    pre = jnp.zeros((inputs.shape[0], H), jnp.float32)
    pre, unused = lax.scan(forward, pre, (grow, gcol, livef, wb))
    act, slope = gelu_parts(pre)
    dpre = (grad_act * slope).astype(jnp.bfloat16)

    def backward(grad_x, item):
        row_one, col_one, live_one, weight = item
        rstart = (row_one * BS).astype(jnp.int32)
        xs = lax.dynamic_slice_in_dim(xb, rstart, BS, 1)
        ds = lax.dynamic_slice_in_dim(dpre, (col_one * BS).astype(jnp.int32), BS, 1)
        part = jnp.dot(ds, weight.T, preferred_element_type=jnp.float32) * live_one
        current = lax.dynamic_slice_in_dim(grad_x, rstart, BS, 1)
        grad_x = lax.dynamic_update_slice_in_dim(grad_x, current + part, rstart, 1)
        wgrad = jnp.dot(xs.T, ds, preferred_element_type=jnp.float32) * live_one
        return grad_x, wgrad

    grad_x = jnp.zeros((inputs.shape[0], D), jnp.float32)
    grad_x, grad_w = lax.scan(backward, grad_x, (grow, gcol, livef, wb))
    return act, grad_x, grad_w
```

```python
import jax
import jax.numpy as jnp
from jax import lax
from jax.experimental import pallas as pl
from jax.experimental.pallas import tpu as pltpu
from jax.sharding import PartitionSpec as P

BS = 128
NY, NX, NC = 8, 4, 2
NZ = 12
HALF = NY * NX
Y_GROUPS = [[(y * NX + x) * NC + c for y in range(NY)] for x in range(NX) for c in range(NC)]
X_GROUPS = [[(y * NX + x) * NC + c for x in range(NX)] for y in range(NY) for c in range(NC)]
CORE_SWAP = [(i, i ^ 1) for i in range(HALF * NC)]
Z_NEAR = [[3 * i + j for j in range(3)] for i in range(4)]
Z_FAR = [[3 * i + j for i in range(4)] for j in range(3)]
F32, BF16 = jnp.float32, jnp.bfloat16


def gelu_parts(pre):
    inner = 0.7978845608 * (pre + 0.044715 * pre * pre * pre)
    tanh_val = jnp.tanh(inner)
    value = 0.5 * pre * (1.0 + tanh_val)
    slope = 0.5 * (1.0 + tanh_val) + 0.5 * pre * (1.0 - tanh_val * tanh_val) * 0.7978845608 * (
        1.0 + 3.0 * 0.044715 * pre * pre
    )
    return value, slope


def dot(a, b, dims):
    return lax.dot_general(a, b, (dims, ((), ())), preferred_element_type=F32)


def block_kernel(idx_ref, col_ref, live_ref, own_ref, sib_ref, w_ref, g_ref,
                 act_ref, gx_own_ref, gx_sib_ref, gw_ref, x_ref, prod_ref, pre_ref, dpre_ref, gx_ref):
    slots = w_ref.shape[0]
    col_blocks = pre_ref.shape[0]
    x_ref[:HALF] = own_ref[...]
    x_ref[HALF:] = sib_ref[...]
    pre_ref[...] = jnp.zeros_like(pre_ref)
    for s in range(slots):
        prod_ref[s] = dot(x_ref[idx_ref[s]], w_ref[s], ((1,), (0,)))
    for s in range(slots):
        pre_ref[col_ref[s]] += prod_ref[s]
    for c in range(col_blocks):
        value, slope = gelu_parts(pre_ref[c])
        lanes = slice(c * BS, (c + 1) * BS)
        act_ref[:, lanes] = value
        dpre_ref[c] = (g_ref[:, lanes] * slope).astype(BF16)
    for s in range(slots):
        wgrad = dot(x_ref[idx_ref[s]], dpre_ref[col_ref[s]], ((0,), (0,)))
        gw_ref[s] = (wgrad * live_ref[s]).astype(BF16)
    gw_ref[slots] = jnp.zeros((BS, BS), BF16)
    gx_ref[...] = jnp.zeros_like(gx_ref)
    for s in range(slots):
        prod_ref[s] = dot(dpre_ref[col_ref[s]], w_ref[s], ((1,), (1,)))
    for s in range(slots):
        gx_ref[idx_ref[s]] += prod_ref[s]
    gx_own_ref[...] = gx_ref[:HALF].astype(BF16)
    gx_sib_ref[...] = gx_ref[HALF:].astype(BF16)


def run_blocks(idx, col, live, own, sib, wb, grad_act):
    slots = wb.shape[0]
    tokens, hidden = grad_act.shape
    smem = pl.BlockSpec(memory_space=pltpu.SMEM)
    vmem = pl.BlockSpec(memory_space=pltpu.VMEM)
    return pl.pallas_call(
        block_kernel,
        out_shape=(
            jax.ShapeDtypeStruct((tokens, hidden), F32),
            jax.ShapeDtypeStruct((HALF, tokens, BS), BF16),
            jax.ShapeDtypeStruct((HALF, tokens, BS), BF16),
            jax.ShapeDtypeStruct((slots + 1, BS, BS), BF16),
        ),
        in_specs=[smem] * 3 + [vmem] * 4,
        out_specs=(vmem,) * 4,
        scratch_shapes=[
            pltpu.VMEM((2 * HALF, tokens, BS), BF16),
            pltpu.VMEM((slots, tokens, BS), F32),
            pltpu.VMEM((hidden // BS, tokens, BS), F32),
            pltpu.VMEM((hidden // BS, tokens, BS), BF16),
            pltpu.VMEM((2 * HALF, tokens, BS), F32),
        ],
        compiler_params=pltpu.CompilerParams(vmem_limit_bytes=40 << 20),
    )(idx, col, live, own, sib, wb, grad_act)


def swap(x, axis, groups):
    return lax.all_to_all(x, axis, 0, 0, tiled=True, axis_index_groups=groups)


def total(x):
    return jnp.sum(x.astype(F32), axis=0)


def local(inputs, block_weights, block_list, grad_act):
    tokens = inputs.shape[0]
    slots = block_weights.shape[0]
    row_ids, col_ids = block_list[:, 0], block_list[:, 1]
    live = (row_ids >= 0).astype(F32)
    row = jnp.maximum(row_ids, 0)
    col = jnp.maximum(col_ids, 0)
    core = lax.axis_index("mp") % NC
    idx = ((row % NC) ^ core) * HALF + ((row // NC) % NX) * NY + row // (NC * NX)
    xb = inputs.astype(BF16)
    wb = (block_weights * live[:, None, None]).astype(BF16)

    by_y = swap(jnp.broadcast_to(xb[None], (NY, tokens, BS)), "mp", Y_GROUPS)
    by_xy = swap(jnp.broadcast_to(by_y[None], (NX, NY, tokens, BS)), "mp", X_GROUPS)
    own = by_xy.reshape(HALF, tokens, BS)
    sib = lax.ppermute(own, "mp", CORE_SWAP)

    act, gx_own, gx_sib, gw = run_blocks(idx, col, live, own, sib, wb, grad_act)

    rows = gw.shape[0] * BS
    near = swap(gw.reshape(3, rows // 3, BS), "dp", Z_NEAR)
    near = total(near).astype(BF16)
    far = swap(near.reshape(4, rows // NZ, BS), "dp", Z_FAR)
    mine = total(far).astype(BF16)
    whole = lax.all_gather(mine, "dp", axis=0, tiled=False)
    whole = whole.reshape(4, 3, rows // NZ, BS).swapaxes(0, 1)
    grad_w = whole.reshape(rows // BS, BS, BS)[:slots].astype(F32)

    gx = (gx_own.astype(F32) + lax.ppermute(gx_sib, "mp", CORE_SWAP).astype(F32)).astype(BF16)
    gx = swap(gx.reshape(NX, NY, tokens, BS), "mp", X_GROUPS)
    gx = swap(total(gx).astype(BF16), "mp", Y_GROUPS)
    grad_x = total(gx)
    return act, grad_x, grad_w


def solution(mesh):
    in_specs = (P("dp", "mp"), P("mp", None, None), P("mp", None), P("dp", "mp"))
    out_specs = (P("dp", "mp"), P("dp", "mp"), P("mp", None, None))
    return jax.shard_map(local, mesh=mesh, in_specs=in_specs, out_specs=out_specs, check_vma=False)
```

```python
import jax
import jax.numpy as jnp
from jax import lax
from jax.experimental import pallas as pl
from jax.experimental.pallas import tpu as pltpu
from jax.sharding import PartitionSpec as P

BS = 128
NY, NX, NC = 8, 4, 2
NZ = 12
HALF = NY * NX
Y_GROUPS = [[(y * NX + x) * NC + c for y in range(NY)] for x in range(NX) for c in range(NC)]
X_GROUPS = [[(y * NX + x) * NC + c for x in range(NX)] for y in range(NY) for c in range(NC)]
CORE_SWAP = [(i, i ^ 1) for i in range(HALF * NC)]
CHUNK = 416
SPLIT = 208
F32, BF16 = jnp.float32, jnp.bfloat16


def gelu_parts(pre):
    inner = 0.7978845608 * (pre + 0.044715 * pre * pre * pre)
    tanh_val = jnp.tanh(inner)
    value = 0.5 * pre * (1.0 + tanh_val)
    slope = 0.5 * (1.0 + tanh_val) + 0.5 * pre * (1.0 - tanh_val * tanh_val) * 0.7978845608 * (
        1.0 + 3.0 * 0.044715 * pre * pre
    )
    return value, slope


def dot(a, b, dims):
    return lax.dot_general(a, b, (dims, ((), ())), preferred_element_type=F32)


def block_kernel(idx_ref, col_ref, live_ref, rel_ref, own_ref, sib_ref, w_ref, g_ref,
                 act_ref, gx_own_ref, gx_sib_ref, keep_ref, up1_ref, down1_ref, up2_ref, down2_ref,
                 x_ref, prod_ref, pre_ref, dpre_ref, gx_ref, gw_ref):
    slots = w_ref.shape[0]
    col_blocks = pre_ref.shape[0]
    x_ref[:HALF] = own_ref[...]
    x_ref[HALF:] = sib_ref[...]
    pre_ref[...] = jnp.zeros_like(pre_ref)
    for s in range(slots):
        prod_ref[s] = dot(x_ref[idx_ref[s]], w_ref[s], ((1,), (0,)))
    for s in range(slots):
        pre_ref[col_ref[s]] += prod_ref[s]
    for c in range(col_blocks):
        value, slope = gelu_parts(pre_ref[c])
        lanes = slice(c * BS, (c + 1) * BS)
        act_ref[:, lanes] = value
        dpre_ref[c] = (g_ref[:, lanes] * slope).astype(BF16)
    for s in range(slots):
        wgrad = dot(x_ref[idx_ref[s]], dpre_ref[col_ref[s]], ((0,), (0,)))
        wgrad = (wgrad * live_ref[s]).astype(BF16)
        done = 0
        while done < BS:
            chunk, at = divmod(s * BS + done, CHUNK)
            size = min(BS - done, CHUNK - at)
            gw_ref[rel_ref[chunk], at:at + size] = wgrad[done:done + size]
            done += size
    chunk, at = divmod(slots * BS, CHUNK)
    gw_ref[rel_ref[chunk], at:] = jnp.zeros((CHUNK - at, BS), BF16)
    for i in range(3):
        keep_ref[i] = gw_ref[4 * i]
        up1_ref[i] = gw_ref[4 * i + 1]
        down1_ref[i] = gw_ref[(4 * i + 11) % NZ]
        up2_ref[i] = gw_ref[4 * i + 2, :SPLIT]
        down2_ref[i] = gw_ref[(4 * i + 10) % NZ, SPLIT:]
    gx_ref[...] = jnp.zeros_like(gx_ref)
    for s in range(slots):
        prod_ref[s] = dot(dpre_ref[col_ref[s]], w_ref[s], ((1,), (1,)))
    for s in range(slots):
        gx_ref[idx_ref[s]] += prod_ref[s]
    gx_own_ref[...] = gx_ref[:HALF].astype(BF16)
    gx_sib_ref[...] = gx_ref[HALF:].astype(BF16)


def near_kernel(after_ref, keep_ref, a_ref, b_ref, c_ref, d_ref, stay_ref, up_ref, down_ref):
    for i, out in enumerate((stay_ref, up_ref, down_ref)):
        part = keep_ref[i].astype(F32) + a_ref[i].astype(F32) + b_ref[i].astype(F32)
        out[:SPLIT] = (part[:SPLIT] + c_ref[i].astype(F32)).astype(BF16)
        out[SPLIT:] = (part[SPLIT:] + d_ref[i].astype(F32)).astype(BF16)


def far_kernel(after_ref, stay_ref, a_ref, b_ref, out_ref):
    out_ref[...] = (stay_ref[...].astype(F32) + a_ref[...].astype(F32) + b_ref[...].astype(F32)).astype(BF16)


def three_kernel(k0_ref, k4_ref, k8_ref, all_ref, low_ref, high_ref):
    for i, part in enumerate((k0_ref, k4_ref, k8_ref)):
        all_ref[i] = part[...]
        low_ref[i] = part[:SPLIT]
        high_ref[i] = part[SPLIT:]


def x_sum_kernel(after_ref, in_ref, out_ref):
    out_ref[...] = jnp.sum(in_ref[...].astype(F32), axis=0).astype(BF16)


def whole_kernel(rel_ref, after_ref, k0_ref, k4_ref, k8_ref, low1_ref, high1_ref, low2_ref, high2_ref, out_ref, gw_ref):
    gw_ref[0] = k0_ref[...]
    gw_ref[4] = k4_ref[...]
    gw_ref[8] = k8_ref[...]
    for i in range(3):
        gw_ref[(4 * i + 11) % NZ] = low1_ref[i]
        gw_ref[4 * i + 1] = high1_ref[i]
        gw_ref[(4 * i + 10) % NZ, :SPLIT] = low2_ref[i]
        gw_ref[4 * i + 2, SPLIT:] = high2_ref[i]
    rows = out_ref.shape[0]
    for j in range(NZ):
        size = min(CHUNK, rows - j * CHUNK)
        out_ref[j * CHUNK:j * CHUNK + size] = gw_ref[rel_ref[j], :size].astype(F32)


def run_blocks(idx, col, live, rel, own, sib, wb, grad_act):
    slots = wb.shape[0]
    tokens, hidden = grad_act.shape
    smem = pl.BlockSpec(memory_space=pltpu.SMEM)
    vmem = pl.BlockSpec(memory_space=pltpu.VMEM)
    return pl.pallas_call(
        block_kernel,
        out_shape=(
            jax.ShapeDtypeStruct((tokens, hidden), F32),
            jax.ShapeDtypeStruct((HALF, tokens, BS), BF16),
            jax.ShapeDtypeStruct((HALF, tokens, BS), BF16),
        ) + (jax.ShapeDtypeStruct((3, CHUNK, BS), BF16),) * 3
        + (jax.ShapeDtypeStruct((3, SPLIT, BS), BF16),) * 2,
        in_specs=[smem] * 4 + [vmem] * 4,
        out_specs=(vmem,) * 8,
        scratch_shapes=[
            pltpu.VMEM((2 * HALF, tokens, BS), BF16),
            pltpu.VMEM((slots, tokens, BS), F32),
            pltpu.VMEM((hidden // BS, tokens, BS), F32),
            pltpu.VMEM((hidden // BS, tokens, BS), BF16),
            pltpu.VMEM((2 * HALF, tokens, BS), F32),
            pltpu.VMEM((NZ, CHUNK, BS), BF16),
        ],
        compiler_params=pltpu.CompilerParams(vmem_limit_bytes=40 << 20),
    )(idx, col, live, rel, own, sib, wb, grad_act)


def swap(x, axis, groups):
    return lax.all_to_all(x, axis, 0, 0, tiled=True, axis_index_groups=groups)


def total(x):
    return jnp.sum(x.astype(F32), axis=0)


def shift(x, by):
    return lax.ppermute(x, "dp", [(i, (i + by) % NZ) for i in range(NZ)])


def call(kernel, ins, outs, after=None):
    vmem = pl.BlockSpec(memory_space=pltpu.VMEM)
    first = () if after is None else (after,)
    return pl.pallas_call(
        kernel,
        out_shape=outs,
        in_specs=[pl.BlockSpec(memory_space=pl.ANY)] * len(first) + [vmem] * len(ins),
        out_specs=jax.tree.map(lambda _: vmem, outs),
        compiler_params=pltpu.CompilerParams(vmem_limit_bytes=20 << 20),
    )(*first, *ins)


def reduce_gradients(gx_own, gx_sib, keep, up1, down1, up2, down2, rel, slots):
    tokens = gx_own.shape[1]
    one = jax.ShapeDtypeStruct((CHUNK, BS), BF16)
    half = jax.ShapeDtypeStruct((3, SPLIT, BS), BF16)
    parts = shift(up1, 1), shift(down1, -1), shift(up2, 2), shift(down2, -2)
    gx_sib = lax.ppermute(gx_sib, "mp", CORE_SWAP)
    gx = (gx_own.astype(F32) + gx_sib.astype(F32)).astype(BF16)
    stay, up, down = call(near_kernel, (keep, *parts), (one,) * 3, gx)

    far = shift(up, 4), shift(down, -4)
    gx = swap(gx.reshape(NX, NY, tokens, BS), "mp", X_GROUPS)
    mine = call(far_kernel, (stay, *far), one, gx)

    k8, k4 = shift(mine, 4), shift(mine, -4)
    three, low, high = call(
        three_kernel, (mine, k4, k8), (jax.ShapeDtypeStruct((3, CHUNK, BS), BF16), half, half)
    )

    low1, high1, low2, high2 = shift(three, 1), shift(three, -1), shift(low, 2), shift(high, -2)
    gx = call(x_sum_kernel, (gx,), jax.ShapeDtypeStruct((NY, tokens, BS), BF16), three)
    grad_x = total(swap(gx, "mp", Y_GROUPS))
    smem = pl.BlockSpec(memory_space=pltpu.SMEM)
    vmem = pl.BlockSpec(memory_space=pltpu.VMEM)
    grad_w = pl.pallas_call(
        whole_kernel,
        out_shape=jax.ShapeDtypeStruct((slots * BS, BS), F32),
        in_specs=[smem, pl.BlockSpec(memory_space=pl.ANY)] + [vmem] * 7,
        out_specs=vmem,
        scratch_shapes=[pltpu.VMEM((NZ, CHUNK, BS), BF16)],
        compiler_params=pltpu.CompilerParams(vmem_limit_bytes=40 << 20),
    )(rel, grad_x, mine, k4, k8, low1, high1, low2, high2)
    return grad_x, grad_w.reshape(slots, BS, BS)


def local(inputs, block_weights, block_list, grad_act):
    tokens = inputs.shape[0]
    slots = block_weights.shape[0]
    row_ids, col_ids = block_list[:, 0], block_list[:, 1]
    live = (row_ids >= 0).astype(F32)
    row = jnp.maximum(row_ids, 0)
    col = jnp.maximum(col_ids, 0)
    core = lax.axis_index("mp") % NC
    idx = ((row % NC) ^ core) * HALF + ((row // NC) % NX) * NY + row // (NC * NX)
    xb = inputs.astype(BF16)
    wb = (block_weights * live[:, None, None]).astype(BF16)

    by_y = swap(jnp.broadcast_to(xb[None], (NY, tokens, BS)), "mp", Y_GROUPS)
    by_xy = swap(jnp.broadcast_to(by_y[None], (NX, NY, tokens, BS)), "mp", X_GROUPS)
    own = by_xy.reshape(HALF, tokens, BS)
    sib = lax.ppermute(own, "mp", CORE_SWAP)

    rel = (jnp.arange(NZ, dtype=jnp.int32) + NZ - lax.axis_index("dp")) % NZ
    act, gx_own, gx_sib, keep, up1, down1, up2, down2 = run_blocks(
        idx, col, live, rel, own, sib, wb, grad_act
    )
    grad_x, grad_w = reduce_gradients(gx_own, gx_sib, keep, up1, down1, up2, down2, rel, slots)
    return act, grad_x, grad_w


def solution(mesh):
    in_specs = (P("dp", "mp"), P("mp", None, None), P("mp", None), P("dp", "mp"))
    out_specs = (P("dp", "mp"), P("dp", "mp"), P("mp", None, None))
    return jax.shard_map(local, mesh=mesh, in_specs=in_specs, out_specs=out_specs, check_vma=False)
```

```python
import jax
import jax.numpy as jnp
from jax import lax
from jax.experimental import pallas as pl
from jax.experimental.pallas import tpu as pltpu
from jax.sharding import PartitionSpec as P

BS = 128
NY, NX, NC = 8, 4, 2
NZ = 12
HALF = NY * NX
Y_GROUPS = [[(y * NX + x) * NC + c for y in range(NY)] for x in range(NX) for c in range(NC)]
X_GROUPS = [[(y * NX + x) * NC + c for x in range(NX)] for y in range(NY) for c in range(NC)]
CORE_SWAP = [(i, i ^ 1) for i in range(HALF * NC)]
CHUNK = 416
Z_FAR = [[3 * i + r for i in range(4)] for r in range(3)]
F32, BF16 = jnp.float32, jnp.bfloat16


def gelu_parts(pre):
    inner = 0.7978845608 * (pre + 0.044715 * pre * pre * pre)
    tanh_val = jnp.tanh(inner)
    value = 0.5 * pre * (1.0 + tanh_val)
    slope = 0.5 * (1.0 + tanh_val) + 0.5 * pre * (1.0 - tanh_val * tanh_val) * 0.7978845608 * (
        1.0 + 3.0 * 0.044715 * pre * pre
    )
    return value, slope


def dot(a, b, dims):
    return lax.dot_general(a, b, (dims, ((), ())), preferred_element_type=F32)


def forward_kernel(idx_ref, col_ref, live_ref, rel_ref, own_ref, sib_ref, w_ref, g_ref,
                   act_ref, dpre_ref, keep_ref, up_ref, down_ref, x_ref, prod_ref, pre_ref, gw_ref):
    slots = w_ref.shape[0]
    x_ref[:HALF] = own_ref[...]
    x_ref[HALF:] = sib_ref[...]
    pre_ref[...] = jnp.zeros_like(pre_ref)
    for s in range(slots):
        prod_ref[s] = dot(x_ref[idx_ref[s]], w_ref[s], ((1,), (0,)))
    for s in range(slots):
        pre_ref[col_ref[s]] += prod_ref[s]
    for c in range(pre_ref.shape[0]):
        value, slope = gelu_parts(pre_ref[c])
        lanes = slice(c * BS, (c + 1) * BS)
        act_ref[:, lanes] = value
        dpre_ref[c] = (g_ref[:, lanes] * slope).astype(BF16)
    for s in range(slots):
        wgrad = dot(x_ref[idx_ref[s]], dpre_ref[col_ref[s]], ((0,), (0,)))
        wgrad = (wgrad * live_ref[s]).astype(BF16)
        done = 0
        while done < BS:
            chunk, at = divmod(s * BS + done, CHUNK)
            size = min(BS - done, CHUNK - at)
            gw_ref[rel_ref[chunk], at:at + size] = wgrad[done:done + size]
            done += size
    chunk, at = divmod(slots * BS, CHUNK)
    gw_ref[rel_ref[chunk], at:] = jnp.zeros((CHUNK - at, BS), BF16)
    for b in range(4):
        keep_ref[b] = gw_ref[3 * b]
        up_ref[b] = gw_ref[3 * b + 1]
        down_ref[b] = gw_ref[(3 * b + 11) % NZ]


def backward_kernel(idx_ref, col_ref, w_ref, dpre_ref, gx_own_ref, gx_sib_ref, prod_ref, gx_ref):
    slots = w_ref.shape[0]
    gx_ref[...] = jnp.zeros_like(gx_ref)
    for s in range(slots):
        prod_ref[s] = dot(dpre_ref[col_ref[s]], w_ref[s], ((1,), (1,)))
    for s in range(slots):
        gx_ref[idx_ref[s]] += prod_ref[s]
    gx_own_ref[...] = gx_ref[:HALF].astype(BF16)
    gx_sib_ref[...] = gx_ref[HALF:].astype(BF16)


def near_kernel(far_ref, after_ref, keep_ref, a_ref, b_ref, out_ref):
    for b in range(4):
        part = keep_ref[b].astype(F32) + a_ref[b].astype(F32) + b_ref[b].astype(F32)
        out_ref[far_ref[b]] = part.astype(BF16)


def far_kernel(after_ref, in_ref, out_ref):
    part = jnp.sum(in_ref[...].astype(F32), axis=0).astype(BF16)
    for b in range(4):
        out_ref[b] = part


def x_sum_kernel(in_ref, out_ref):
    out_ref[...] = jnp.sum(in_ref[...].astype(F32), axis=0).astype(BF16)


def whole_kernel(place_ref, after_ref, mid_ref, low_ref, high_ref, out_ref, gw_ref):
    for i, part in enumerate((low_ref, mid_ref, high_ref)):
        for b in range(4):
            gw_ref[3 * b + place_ref[i]] = part[b]
    rows = out_ref.shape[0]
    for j in range(NZ):
        size = min(CHUNK, rows - j * CHUNK)
        out_ref[j * CHUNK:j * CHUNK + size] = gw_ref[j, :size].astype(F32)


SMEM = pl.BlockSpec(memory_space=pltpu.SMEM)
VMEM = pl.BlockSpec(memory_space=pltpu.VMEM)
ORDER = pl.BlockSpec(memory_space=pl.ANY)


def call(kernel, specs, ins, outs, scratch=(), flops=0, moved=0):
    return pl.pallas_call(
        kernel,
        out_shape=outs,
        in_specs=specs,
        out_specs=jax.tree.map(lambda _: VMEM, outs),
        scratch_shapes=scratch,
        compiler_params=pltpu.CompilerParams(vmem_limit_bytes=40 << 20),
        cost_estimate=pl.CostEstimate(flops=flops, bytes_accessed=moved, transcendentals=0),
    )(*ins)


def array(shape, kind=BF16):
    return jax.ShapeDtypeStruct(shape, kind)


def forward(idx, col, live, rel, own, sib, wb, grad_act):
    slots = wb.shape[0]
    tokens, hidden = grad_act.shape
    cols = hidden // BS
    chunks = array((4, CHUNK, BS))
    return call(
        forward_kernel,
        [SMEM] * 4 + [VMEM] * 4,
        (idx, col, live, rel, own, sib, wb, grad_act),
        (array((tokens, hidden), F32), array((cols, tokens, BS)), chunks, chunks, chunks),
        [
            pltpu.VMEM((2 * HALF, tokens, BS), BF16),
            pltpu.VMEM((slots, tokens, BS), F32),
            pltpu.VMEM((cols, tokens, BS), F32),
            pltpu.VMEM((NZ, CHUNK, BS), BF16),
        ],
    )


def backward(idx, col, wb, dpre):
    slots = wb.shape[0]
    tokens = dpre.shape[1]
    half = array((HALF, tokens, BS))
    return call(
        backward_kernel,
        [SMEM] * 2 + [VMEM] * 2,
        (idx, col, wb, dpre),
        (half, half),
        [pltpu.VMEM((slots, tokens, BS), F32), pltpu.VMEM((2 * HALF, tokens, BS), F32)],
        flops=2 * slots * tokens * BS * BS,
        moved=8 << 20,
    )


def swap(x, axis, groups):
    return lax.all_to_all(x, axis, 0, 0, tiled=True, axis_index_groups=groups)


def total(x):
    return jnp.sum(x.astype(F32), axis=0)


def shift(x, by):
    return lax.ppermute(x, "dp", [(i, (i + by) % NZ) for i in range(NZ)])


def reduce_gradients(gx_own, gx_sib, keep, up, down, slots):
    tokens = gx_own.shape[1]
    z = lax.axis_index("dp")
    chunks = array((4, CHUNK, BS))
    from_low, from_high = shift(up, 1), shift(down, -1)
    gx_sib = lax.ppermute(gx_sib, "mp", CORE_SWAP)
    gx = (gx_own.astype(F32) + gx_sib.astype(F32)).astype(BF16)
    member = (jnp.arange(4, dtype=jnp.int32) + z // 3) % 4
    near = call(
        near_kernel, [SMEM, ORDER] + [VMEM] * 3, (member, gx, keep, from_low, from_high), chunks
    )

    far = swap(near, "dp", Z_FAR)
    gx = swap(gx.reshape(NX, NY, tokens, BS), "mp", X_GROUPS)
    mine = call(far_kernel, [ORDER, VMEM], (gx, far), chunks)

    mid = swap(mine, "dp", Z_FAR)
    gx = call(x_sum_kernel, [VMEM], (gx,), array((NY, tokens, BS)))
    grad_x = total(swap(gx, "mp", Y_GROUPS))

    low, high = shift(mid, 1), shift(mid, -1)
    place = (jnp.arange(3, dtype=jnp.int32) + z + 2) % 3
    grad_w = call(
        whole_kernel,
        [SMEM, ORDER] + [VMEM] * 3,
        (place, grad_x, mid, low, high),
        array((slots * BS, BS), F32),
        [pltpu.VMEM((NZ, CHUNK, BS), BF16)],
    )
    return grad_x, grad_w.reshape(slots, BS, BS)


def local(inputs, block_weights, block_list, grad_act):
    tokens = inputs.shape[0]
    slots = block_weights.shape[0]
    row_ids, col_ids = block_list[:, 0], block_list[:, 1]
    live = (row_ids >= 0).astype(F32)
    row = jnp.maximum(row_ids, 0)
    col = jnp.maximum(col_ids, 0)
    core = lax.axis_index("mp") % NC
    idx = ((row % NC) ^ core) * HALF + ((row // NC) % NX) * NY + row // (NC * NX)
    xb = inputs.astype(BF16)
    wb = (block_weights * live[:, None, None]).astype(BF16)

    by_y = swap(jnp.broadcast_to(xb[None], (NY, tokens, BS)), "mp", Y_GROUPS)
    by_xy = swap(jnp.broadcast_to(by_y[None], (NX, NY, tokens, BS)), "mp", X_GROUPS)
    own = by_xy.reshape(HALF, tokens, BS)
    sib = lax.ppermute(own, "mp", CORE_SWAP)

    rel = (jnp.arange(NZ, dtype=jnp.int32) + NZ - lax.axis_index("dp")) % NZ
    act, dpre, keep, up, down = forward(idx, col, live, rel, own, sib, wb, grad_act)
    gx_own, gx_sib = backward(idx, col, wb, dpre)
    grad_x, grad_w = reduce_gradients(gx_own, gx_sib, keep, up, down, slots)
    return act, grad_x, grad_w


def solution(mesh):
    in_specs = (P("dp", "mp"), P("mp", None, None), P("mp", None), P("dp", "mp"))
    out_specs = (P("dp", "mp"), P("dp", "mp"), P("mp", None, None))
    return jax.shard_map(local, mesh=mesh, in_specs=in_specs, out_specs=out_specs, check_vma=False)
```

```python
import jax
import jax.numpy as jnp
from jax import lax
from jax.experimental import pallas as pl
from jax.experimental.pallas import tpu as pltpu
from jax.sharding import PartitionSpec as P

BS = 128
NY, NX, NC = 8, 4, 2
NZ = 12
HALF = NY * NX
Y_GROUPS = [[(y * NX + x) * NC + c for y in range(NY)] for x in range(NX) for c in range(NC)]
X_GROUPS = [[(y * NX + x) * NC + c for x in range(NX)] for y in range(NY) for c in range(NC)]
CORE_SWAP = [(i, i ^ 1) for i in range(HALF * NC)]
XC_GROUPS = [[y * NX * NC + k for k in range(NX * NC)] for y in range(NY)]
CHUNK = 416
SPLIT = 208
F32, BF16 = jnp.float32, jnp.bfloat16


def gelu_parts(pre):
    inner = 0.7978845608 * (pre + 0.044715 * pre * pre * pre)
    tanh_val = jnp.tanh(inner)
    value = 0.5 * pre * (1.0 + tanh_val)
    slope = 0.5 * (1.0 + tanh_val) + 0.5 * pre * (1.0 - tanh_val * tanh_val) * 0.7978845608 * (
        1.0 + 3.0 * 0.044715 * pre * pre
    )
    return value, slope


def dot(a, b, dims):
    return lax.dot_general(a, b, (dims, ((), ())), preferred_element_type=F32)


def block_kernel(idx_ref, out_idx_ref, col_ref, live_ref, rel_ref, own_ref, sib_ref, w_ref, g_ref,
                 act_ref, gx_out_ref, keep_ref, up1_ref, down1_ref, up2_ref, down2_ref,
                 x_ref, prod_ref, pre_ref, dpre_ref, gx_ref, gw_ref):
    slots = w_ref.shape[0]
    col_blocks = pre_ref.shape[0]
    x_ref[:HALF] = own_ref[...]
    x_ref[HALF:] = sib_ref[...]
    pre_ref[...] = jnp.zeros_like(pre_ref)
    for s in range(slots):
        prod_ref[s] = dot(x_ref[idx_ref[s]], w_ref[s], ((1,), (0,)))
    for s in range(slots):
        pre_ref[col_ref[s]] += prod_ref[s]
    for c in range(col_blocks):
        value, slope = gelu_parts(pre_ref[c])
        lanes = slice(c * BS, (c + 1) * BS)
        act_ref[:, lanes] = value
        dpre_ref[c] = (g_ref[:, lanes] * slope).astype(BF16)
    for s in range(slots):
        wgrad = dot(x_ref[idx_ref[s]], dpre_ref[col_ref[s]], ((0,), (0,)))
        wgrad = (wgrad * live_ref[s]).astype(BF16)
        done = 0
        while done < BS:
            chunk, at = divmod(s * BS + done, CHUNK)
            size = min(BS - done, CHUNK - at)
            gw_ref[rel_ref[chunk], at:at + size] = wgrad[done:done + size]
            done += size
    chunk, at = divmod(slots * BS, CHUNK)
    gw_ref[rel_ref[chunk], at:] = jnp.zeros((CHUNK - at, BS), BF16)
    for i in range(3):
        keep_ref[i] = gw_ref[4 * i]
        up1_ref[i] = gw_ref[4 * i + 1]
        down1_ref[i] = gw_ref[(4 * i + 11) % NZ]
        up2_ref[i] = gw_ref[4 * i + 2, :SPLIT]
        down2_ref[i] = gw_ref[(4 * i + 10) % NZ, SPLIT:]
    gx_ref[...] = jnp.zeros_like(gx_ref)
    for s in range(slots):
        prod_ref[s] = dot(dpre_ref[col_ref[s]], w_ref[s], ((1,), (1,)))
    for s in range(slots):
        gx_ref[out_idx_ref[s]] += prod_ref[s]
    gx_out_ref[...] = gx_ref[...].astype(BF16)


def near_kernel(keep_ref, a_ref, b_ref, c_ref, d_ref, stay_ref, up_ref, down_ref):
    for i, out in enumerate((stay_ref, up_ref, down_ref)):
        part = keep_ref[i].astype(F32) + a_ref[i].astype(F32) + b_ref[i].astype(F32)
        out[:SPLIT] = (part[:SPLIT] + c_ref[i].astype(F32)).astype(BF16)
        out[SPLIT:] = (part[SPLIT:] + d_ref[i].astype(F32)).astype(BF16)


def far_kernel(stay_ref, a_ref, b_ref, out_ref):
    out_ref[...] = (stay_ref[...].astype(F32) + a_ref[...].astype(F32) + b_ref[...].astype(F32)).astype(BF16)


def three_kernel(after_ref, k0_ref, k4_ref, k8_ref, all_ref, low_ref, high_ref):
    for i, part in enumerate((k0_ref, k4_ref, k8_ref)):
        all_ref[i] = part[...]
        low_ref[i] = part[:SPLIT]
        high_ref[i] = part[SPLIT:]


def x_sum_kernel(after_ref, in_ref, out_ref):
    out_ref[...] = jnp.sum(in_ref[...].astype(F32), axis=0).astype(BF16)


def whole_kernel(rel_ref, k0_ref, k4_ref, k8_ref, low1_ref, high1_ref, low2_ref, high2_ref, out_ref, gw_ref):
    gw_ref[0] = k0_ref[...]
    gw_ref[4] = k4_ref[...]
    gw_ref[8] = k8_ref[...]
    for i in range(3):
        gw_ref[(4 * i + 11) % NZ] = low1_ref[i]
        gw_ref[4 * i + 1] = high1_ref[i]
        gw_ref[(4 * i + 10) % NZ, :SPLIT] = low2_ref[i]
        gw_ref[4 * i + 2, SPLIT:] = high2_ref[i]
    rows = out_ref.shape[0]
    for j in range(NZ):
        size = min(CHUNK, rows - j * CHUNK)
        out_ref[j * CHUNK:j * CHUNK + size] = gw_ref[rel_ref[j], :size].astype(F32)


SMEM = pl.BlockSpec(memory_space=pltpu.SMEM)
VMEM = pl.BlockSpec(memory_space=pltpu.VMEM)
ORDER = pl.BlockSpec(memory_space=pl.ANY)


def call(kernel, specs, ins, outs, scratch=(), flops=0, moved=0):
    return pl.pallas_call(
        kernel,
        out_shape=outs,
        in_specs=specs,
        out_specs=jax.tree.map(lambda _: VMEM, outs),
        scratch_shapes=scratch,
        compiler_params=pltpu.CompilerParams(vmem_limit_bytes=40 << 20),
        cost_estimate=pl.CostEstimate(flops=flops, bytes_accessed=moved, transcendentals=0),
    )(*ins)


def array(shape, kind=BF16):
    return jax.ShapeDtypeStruct(shape, kind)


def run_blocks(idx, out_idx, col, live, rel, own, sib, wb, grad_act):
    slots = wb.shape[0]
    tokens, hidden = grad_act.shape
    cols = hidden // BS
    full, half = array((3, CHUNK, BS)), array((3, SPLIT, BS))
    return call(
        block_kernel,
        [SMEM] * 5 + [VMEM] * 4,
        (idx, out_idx, col, live, rel, own, sib, wb, grad_act),
        (array((tokens, hidden), F32), array((2 * HALF, tokens, BS)), full, full, full, half, half),
        [
            pltpu.VMEM((2 * HALF, tokens, BS), BF16),
            pltpu.VMEM((slots, tokens, BS), F32),
            pltpu.VMEM((cols, tokens, BS), F32),
            pltpu.VMEM((cols, tokens, BS), BF16),
            pltpu.VMEM((2 * HALF, tokens, BS), F32),
            pltpu.VMEM((NZ, CHUNK, BS), BF16),
        ],
    )


def swap(x, axis, groups):
    return lax.all_to_all(x, axis, 0, 0, tiled=True, axis_index_groups=groups)


def total(x):
    return jnp.sum(x.astype(F32), axis=0)


def shift(x, by):
    return lax.ppermute(x, "dp", [(i, (i + by) % NZ) for i in range(NZ)])


def reduce_gradients(gx, keep, up1, down1, up2, down2, rel, slots):
    tokens = gx.shape[1]
    one, full, half = array((CHUNK, BS)), array((3, CHUNK, BS)), array((3, SPLIT, BS))
    gx = swap(gx.reshape(NX * NC, NY, tokens, BS), "mp", XC_GROUPS)
    parts = shift(up1, 1), shift(down1, -1), shift(up2, 2), shift(down2, -2)
    stay, up, down = call(near_kernel, [VMEM] * 5, (keep, *parts), (one,) * 3)
    mine = call(far_kernel, [VMEM] * 3, (stay, shift(up, 4), shift(down, -4)), one)

    k8, k4 = shift(mine, 4), shift(mine, -4)
    gx = call(x_sum_kernel, [ORDER, VMEM], (mine, gx), array((NY, tokens, BS)))
    three, low, high = call(three_kernel, [ORDER] + [VMEM] * 3, (gx, mine, k4, k8), (full, half, half))
    grad_x = total(swap(gx, "mp", Y_GROUPS))

    low1, high1, low2, high2 = shift(three, 1), shift(three, -1), shift(low, 2), shift(high, -2)
    grad_w = call(
        whole_kernel,
        [SMEM] + [VMEM] * 7,
        (rel, mine, k4, k8, low1, high1, low2, high2),
        array((slots * BS, BS), F32),
        [pltpu.VMEM((NZ, CHUNK, BS), BF16)],
    )
    return grad_x, grad_w.reshape(slots, BS, BS)


def local(inputs, block_weights, block_list, grad_act):
    tokens = inputs.shape[0]
    slots = block_weights.shape[0]
    row_ids, col_ids = block_list[:, 0], block_list[:, 1]
    live = (row_ids >= 0).astype(F32)
    row = jnp.maximum(row_ids, 0)
    col = jnp.maximum(col_ids, 0)
    core = lax.axis_index("mp") % NC
    at_y, at_x, at_core = row // (NC * NX), (row // NC) % NX, row % NC
    idx = ((at_core ^ core) * NX + at_x) * NY + at_y
    out_idx = (at_x * NC + at_core) * NY + at_y
    xb = inputs.astype(BF16)
    wb = (block_weights * live[:, None, None]).astype(BF16)

    by_y = swap(jnp.broadcast_to(xb[None], (NY, tokens, BS)), "mp", Y_GROUPS)
    by_xy = swap(jnp.broadcast_to(by_y[None], (NX, NY, tokens, BS)), "mp", X_GROUPS)
    own = by_xy.reshape(HALF, tokens, BS)
    sib = lax.ppermute(own, "mp", CORE_SWAP)

    rel = (jnp.arange(NZ, dtype=jnp.int32) + NZ - lax.axis_index("dp")) % NZ
    act, gx, *parts = run_blocks(idx, out_idx, col, live, rel, own, sib, wb, grad_act)
    grad_x, grad_w = reduce_gradients(gx, *parts, rel, slots)
    return act, grad_x, grad_w


def solution(mesh):
    in_specs = (P("dp", "mp"), P("mp", None, None), P("mp", None), P("dp", "mp"))
    out_specs = (P("dp", "mp"), P("dp", "mp"), P("mp", None, None))
    return jax.shard_map(local, mesh=mesh, in_specs=in_specs, out_specs=out_specs, check_vma=False)
```

```python
import jax
import jax.numpy as jnp
from jax import lax
from jax.experimental import pallas as pl
from jax.experimental.pallas import tpu as pltpu
from jax.sharding import PartitionSpec as P

BS = 128
NY, NX, NC = 8, 4, 2
NZ = 12
HALF = NY * NX
Y_GROUPS = [[(y * NX + x) * NC + c for y in range(NY)] for x in range(NX) for c in range(NC)]
X_GROUPS = [[(y * NX + x) * NC + c for x in range(NX)] for y in range(NY) for c in range(NC)]
CORE_SWAP = [(i, i ^ 1) for i in range(HALF * NC)]
XC_GROUPS = [[y * NX * NC + k for k in range(NX * NC)] for y in range(NY)]
CHUNK = 416
SPLIT = 208
F32, BF16 = jnp.float32, jnp.bfloat16


def gelu_parts(pre):
    inner = 0.7978845608 * (pre + 0.044715 * pre * pre * pre)
    tanh_val = jnp.tanh(inner)
    value = 0.5 * pre * (1.0 + tanh_val)
    slope = 0.5 * (1.0 + tanh_val) + 0.5 * pre * (1.0 - tanh_val * tanh_val) * 0.7978845608 * (
        1.0 + 3.0 * 0.044715 * pre * pre
    )
    return value, slope


def dot(a, b, dims):
    return lax.dot_general(a, b, (dims, ((), ())), preferred_element_type=F32)


def block_kernel(idx_ref, out_idx_ref, col_ref, live_ref, rel_ref, own_ref, sib_ref, w_ref, g_ref,
                 act_ref, gx_out_ref, keep_ref, up1_ref, down1_ref, up2_ref, down2_ref,
                 x_ref, prod_ref, pre_ref, dpre_ref, gx_ref, gw_ref):
    slots = w_ref.shape[0]
    col_blocks = pre_ref.shape[0]
    x_ref[:HALF] = own_ref[...]
    x_ref[HALF:] = sib_ref[...]
    pre_ref[...] = jnp.zeros_like(pre_ref)
    for s in range(slots):
        prod_ref[s] = dot(x_ref[idx_ref[s]], w_ref[s], ((1,), (0,)))
    for s in range(slots):
        pre_ref[col_ref[s]] += prod_ref[s]
    for c in range(col_blocks):
        value, slope = gelu_parts(pre_ref[c])
        lanes = slice(c * BS, (c + 1) * BS)
        act_ref[:, lanes] = value
        dpre_ref[c] = (g_ref[:, lanes] * slope).astype(BF16)
    for s in range(slots):
        wgrad = dot(x_ref[idx_ref[s]], dpre_ref[col_ref[s]], ((0,), (0,)))
        wgrad = (wgrad * live_ref[s]).astype(BF16)
        done = 0
        while done < BS:
            chunk, at = divmod(s * BS + done, CHUNK)
            size = min(BS - done, CHUNK - at)
            gw_ref[rel_ref[chunk], at:at + size] = wgrad[done:done + size]
            done += size
    chunk, at = divmod(slots * BS, CHUNK)
    gw_ref[rel_ref[chunk], at:] = jnp.zeros((CHUNK - at, BS), BF16)
    for i in range(3):
        keep_ref[i] = gw_ref[4 * i]
        up1_ref[i] = gw_ref[4 * i + 1]
        down1_ref[i] = gw_ref[(4 * i + 11) % NZ]
        up2_ref[i] = gw_ref[4 * i + 2, :SPLIT]
        down2_ref[i] = gw_ref[(4 * i + 10) % NZ, SPLIT:]
    gx_ref[...] = jnp.zeros_like(gx_ref)
    for s in range(slots):
        prod_ref[s] = dot(dpre_ref[col_ref[s]], w_ref[s], ((1,), (1,)))
    for s in range(slots):
        gx_ref[out_idx_ref[s]] += prod_ref[s]
    gx_out_ref[...] = gx_ref[...].astype(BF16)


def near_kernel(keep_ref, a_ref, b_ref, c_ref, d_ref, stay_ref, up_ref, down_ref):
    for i, out in enumerate((stay_ref, up_ref, down_ref)):
        part = keep_ref[i].astype(F32) + a_ref[i].astype(F32) + b_ref[i].astype(F32)
        out[:SPLIT] = (part[:SPLIT] + c_ref[i].astype(F32)).astype(BF16)
        out[SPLIT:] = (part[SPLIT:] + d_ref[i].astype(F32)).astype(BF16)


def far_kernel(stay_ref, a_ref, b_ref, low_ref, high_ref):
    part = (stay_ref[...].astype(F32) + a_ref[...].astype(F32) + b_ref[...].astype(F32)).astype(BF16)
    low_ref[...] = part[:SPLIT]
    high_ref[...] = part[SPLIT:]


def x_sum_kernel(after_ref, in_ref, high_ref, out_ref, high_out_ref):
    out_ref[...] = jnp.sum(in_ref[...].astype(F32), axis=0).astype(BF16)
    high_out_ref[...] = high_ref[...]


def whole_kernel(low_ref, high_ref, out_ref):
    rows = out_ref.shape[0]
    for j in range(NZ):
        for half, part in enumerate((low_ref, high_ref)):
            at = j * CHUNK + half * SPLIT
            size = min(SPLIT, rows - at)
            out_ref[at:at + size] = part[j, :size].astype(F32)


SMEM = pl.BlockSpec(memory_space=pltpu.SMEM)
VMEM = pl.BlockSpec(memory_space=pltpu.VMEM)
ORDER = pl.BlockSpec(memory_space=pl.ANY)


def call(kernel, specs, ins, outs, scratch=(), flops=0, moved=0):
    return pl.pallas_call(
        kernel,
        out_shape=outs,
        in_specs=specs,
        out_specs=jax.tree.map(lambda _: VMEM, outs),
        scratch_shapes=scratch,
        compiler_params=pltpu.CompilerParams(vmem_limit_bytes=40 << 20),
        cost_estimate=pl.CostEstimate(flops=flops, bytes_accessed=moved, transcendentals=0),
    )(*ins)


def array(shape, kind=BF16):
    return jax.ShapeDtypeStruct(shape, kind)


def run_blocks(idx, out_idx, col, live, rel, own, sib, wb, grad_act):
    slots = wb.shape[0]
    tokens, hidden = grad_act.shape
    cols = hidden // BS
    full, half = array((3, CHUNK, BS)), array((3, SPLIT, BS))
    return call(
        block_kernel,
        [SMEM] * 5 + [VMEM] * 4,
        (idx, out_idx, col, live, rel, own, sib, wb, grad_act),
        (array((tokens, hidden), F32), array((2 * HALF, tokens, BS)), full, full, full, half, half),
        [
            pltpu.VMEM((2 * HALF, tokens, BS), BF16),
            pltpu.VMEM((slots, tokens, BS), F32),
            pltpu.VMEM((cols, tokens, BS), F32),
            pltpu.VMEM((cols, tokens, BS), BF16),
            pltpu.VMEM((2 * HALF, tokens, BS), F32),
            pltpu.VMEM((NZ, CHUNK, BS), BF16),
        ],
    )


def swap(x, axis, groups):
    return lax.all_to_all(x, axis, 0, 0, tiled=True, axis_index_groups=groups)


def total(x):
    return jnp.sum(x.astype(F32), axis=0)


def shift(x, by):
    return lax.ppermute(x, "dp", [(i, (i + by) % NZ) for i in range(NZ)])


def reduce_gradients(gx, keep, up1, down1, up2, down2, slots):
    tokens = gx.shape[1]
    one = array((CHUNK, BS))
    gx = swap(gx.reshape(NX * NC, NY, tokens, BS), "mp", XC_GROUPS)
    parts = shift(up1, 1), shift(down1, -1), shift(up2, 2), shift(down2, -2)
    stay, up, down = call(near_kernel, [VMEM] * 5, (keep, *parts), (one,) * 3)
    piece = array((SPLIT, BS))
    low, high = call(far_kernel, [VMEM] * 3, (stay, shift(up, 4), shift(down, -4)), (piece, piece))

    low = lax.all_gather(low, "dp")
    gx, high = call(
        x_sum_kernel, [ORDER, VMEM, VMEM], (low, gx, high), (array((NY, tokens, BS)), piece)
    )
    grad_x = total(swap(gx, "mp", Y_GROUPS))
    high = lax.all_gather(high, "dp")
    grad_w = call(whole_kernel, [VMEM] * 2, (low, high), array((slots * BS, BS), F32))
    return grad_x, grad_w.reshape(slots, BS, BS)


def local(inputs, block_weights, block_list, grad_act):
    tokens = inputs.shape[0]
    slots = block_weights.shape[0]
    row_ids, col_ids = block_list[:, 0], block_list[:, 1]
    live = (row_ids >= 0).astype(F32)
    row = jnp.maximum(row_ids, 0)
    col = jnp.maximum(col_ids, 0)
    core = lax.axis_index("mp") % NC
    at_y, at_x, at_core = row // (NC * NX), (row // NC) % NX, row % NC
    idx = ((at_core ^ core) * NX + at_x) * NY + at_y
    out_idx = (at_x * NC + at_core) * NY + at_y
    xb = inputs.astype(BF16)
    wb = (block_weights * live[:, None, None]).astype(BF16)

    by_y = swap(jnp.broadcast_to(xb[None], (NY, tokens, BS)), "mp", Y_GROUPS)
    by_xy = swap(jnp.broadcast_to(by_y[None], (NX, NY, tokens, BS)), "mp", X_GROUPS)
    own = by_xy.reshape(HALF, tokens, BS)
    sib = lax.ppermute(own, "mp", CORE_SWAP)

    rel = (jnp.arange(NZ, dtype=jnp.int32) + NZ - lax.axis_index("dp")) % NZ
    act, gx, *parts = run_blocks(idx, out_idx, col, live, rel, own, sib, wb, grad_act)
    grad_x, grad_w = reduce_gradients(gx, *parts, slots)
    return act, grad_x, grad_w


def solution(mesh):
    in_specs = (P("dp", "mp"), P("mp", None, None), P("mp", None), P("dp", "mp"))
    out_specs = (P("dp", "mp"), P("dp", "mp"), P("mp", None, None))
    return jax.shard_map(local, mesh=mesh, in_specs=in_specs, out_specs=out_specs, check_vma=False)
```

```python
import jax
import jax.numpy as jnp
from jax import lax
from jax.experimental import pallas as pl
from jax.experimental.pallas import tpu as pltpu
from jax.sharding import PartitionSpec as P

BS = 128
NY, NX, NC = 8, 4, 2
NZ = 12
HALF = NY * NX
Y_GROUPS = [[(y * NX + x) * NC + c for y in range(NY)] for x in range(NX) for c in range(NC)]
X_GROUPS = [[(y * NX + x) * NC + c for x in range(NX)] for y in range(NY) for c in range(NC)]
CORE_SWAP = [(i, i ^ 1) for i in range(HALF * NC)]
XC_GROUPS = [[y * NX * NC + k for k in range(NX * NC)] for y in range(NY)]
CHUNK = 416
SPLIT = 208
F32, BF16 = jnp.float32, jnp.bfloat16


def gelu_parts(pre):
    inner = 0.7978845608 * (pre + 0.044715 * pre * pre * pre)
    tanh_val = jnp.tanh(inner)
    value = 0.5 * pre * (1.0 + tanh_val)
    slope = 0.5 * (1.0 + tanh_val) + 0.5 * pre * (1.0 - tanh_val * tanh_val) * 0.7978845608 * (
        1.0 + 3.0 * 0.044715 * pre * pre
    )
    return value, slope


def dot(a, b, dims):
    return lax.dot_general(a, b, (dims, ((), ())), preferred_element_type=F32)


def block_kernel(idx_ref, out_idx_ref, col_ref, live_ref, rel_ref, own_ref, sib_ref, w_ref, g_ref,
                 act_ref, gx_out_ref, keep_ref, up1_ref, down1_ref, up2_ref, down2_ref,
                 x_ref, prod_ref, pre_ref, dpre_ref, gx_ref, gw_ref):
    slots = w_ref.shape[0]
    col_blocks = pre_ref.shape[0]
    x_ref[:HALF] = own_ref[...]
    x_ref[HALF:] = sib_ref[...]
    pre_ref[...] = jnp.zeros_like(pre_ref)
    for s in range(slots):
        prod_ref[s] = dot(x_ref[idx_ref[s]], w_ref[s], ((1,), (0,)))
    for s in range(slots):
        pre_ref[col_ref[s]] += prod_ref[s]
    for c in range(col_blocks):
        value, slope = gelu_parts(pre_ref[c])
        lanes = slice(c * BS, (c + 1) * BS)
        act_ref[:, lanes] = value
        dpre_ref[c] = (g_ref[:, lanes] * slope).astype(BF16)
    for s in range(slots):
        wgrad = dot(x_ref[idx_ref[s]], dpre_ref[col_ref[s]], ((0,), (0,)))
        wgrad = (wgrad * live_ref[s]).astype(BF16)
        done = 0
        while done < BS:
            chunk, at = divmod(s * BS + done, CHUNK)
            size = min(BS - done, CHUNK - at)
            gw_ref[rel_ref[chunk], at:at + size] = wgrad[done:done + size]
            done += size
    chunk, at = divmod(slots * BS, CHUNK)
    gw_ref[rel_ref[chunk], at:] = jnp.zeros((CHUNK - at, BS), BF16)
    for i in range(3):
        keep_ref[i] = gw_ref[4 * i]
        up1_ref[i] = gw_ref[4 * i + 1]
        down1_ref[i] = gw_ref[(4 * i + 11) % NZ]
        up2_ref[i] = gw_ref[4 * i + 2, :SPLIT]
        down2_ref[i] = gw_ref[(4 * i + 10) % NZ, SPLIT:]
    gx_ref[...] = jnp.zeros_like(gx_ref)
    for s in range(slots):
        prod_ref[s] = dot(dpre_ref[col_ref[s]], w_ref[s], ((1,), (1,)))
    for s in range(slots):
        gx_ref[out_idx_ref[s]] += prod_ref[s]
    gx_out_ref[...] = gx_ref[...].astype(BF16)


def near_kernel(keep_ref, a_ref, b_ref, c_ref, d_ref, stay_ref, up_ref, down_ref):
    for i, out in enumerate((stay_ref, up_ref, down_ref)):
        part = keep_ref[i].astype(F32) + a_ref[i].astype(F32) + b_ref[i].astype(F32)
        out[:SPLIT] = (part[:SPLIT] + c_ref[i].astype(F32)).astype(BF16)
        out[SPLIT:] = (part[SPLIT:] + d_ref[i].astype(F32)).astype(BF16)


def far_kernel(stay_ref, a_ref, b_ref, out_ref):
    out_ref[...] = (stay_ref[...].astype(F32) + a_ref[...].astype(F32) + b_ref[...].astype(F32)).astype(BF16)


def four_kernel(after_ref, k0_ref, k3_ref, k6_ref, k9_ref, out_ref):
    for i, part in enumerate((k0_ref, k3_ref, k6_ref, k9_ref)):
        out_ref[i] = part[...]


def x_sum_kernel(after_ref, in_ref, out_ref):
    out_ref[...] = jnp.sum(in_ref[...].astype(F32), axis=0).astype(BF16)


def whole_kernel(rel_ref, after_ref, mid_ref, low_ref, high_ref, out_ref, gw_ref):
    for i in range(4):
        gw_ref[3 * i] = mid_ref[i]
        gw_ref[(3 * i + 11) % NZ] = low_ref[i]
        gw_ref[3 * i + 1] = high_ref[i]
    rows = out_ref.shape[0]
    for j in range(NZ):
        size = min(CHUNK, rows - j * CHUNK)
        out_ref[j * CHUNK:j * CHUNK + size] = gw_ref[rel_ref[j], :size].astype(F32)


SMEM = pl.BlockSpec(memory_space=pltpu.SMEM)
VMEM = pl.BlockSpec(memory_space=pltpu.VMEM)
ORDER = pl.BlockSpec(memory_space=pl.ANY)


def call(kernel, specs, ins, outs, scratch=(), flops=0, moved=0):
    return pl.pallas_call(
        kernel,
        out_shape=outs,
        in_specs=specs,
        out_specs=jax.tree.map(lambda _: VMEM, outs),
        scratch_shapes=scratch,
        compiler_params=pltpu.CompilerParams(vmem_limit_bytes=40 << 20),
        cost_estimate=pl.CostEstimate(flops=flops, bytes_accessed=moved, transcendentals=0),
    )(*ins)


def array(shape, kind=BF16):
    return jax.ShapeDtypeStruct(shape, kind)


def run_blocks(idx, out_idx, col, live, rel, own, sib, wb, grad_act):
    slots = wb.shape[0]
    tokens, hidden = grad_act.shape
    cols = hidden // BS
    full, half = array((3, CHUNK, BS)), array((3, SPLIT, BS))
    return call(
        block_kernel,
        [SMEM] * 5 + [VMEM] * 4,
        (idx, out_idx, col, live, rel, own, sib, wb, grad_act),
        (array((tokens, hidden), F32), array((2 * HALF, tokens, BS)), full, full, full, half, half),
        [
            pltpu.VMEM((2 * HALF, tokens, BS), BF16),
            pltpu.VMEM((slots, tokens, BS), F32),
            pltpu.VMEM((cols, tokens, BS), F32),
            pltpu.VMEM((cols, tokens, BS), BF16),
            pltpu.VMEM((2 * HALF, tokens, BS), F32),
            pltpu.VMEM((NZ, CHUNK, BS), BF16),
        ],
    )


def swap(x, axis, groups):
    return lax.all_to_all(x, axis, 0, 0, tiled=True, axis_index_groups=groups)


def total(x):
    return jnp.sum(x.astype(F32), axis=0)


def shift(x, by):
    return lax.ppermute(x, "dp", [(i, (i + by) % NZ) for i in range(NZ)])


def reduce_gradients(gx, keep, up1, down1, up2, down2, rel, slots):
    tokens = gx.shape[1]
    one = array((CHUNK, BS))
    gx = swap(gx.reshape(NX * NC, NY, tokens, BS), "mp", XC_GROUPS)
    parts = shift(up1, 1), shift(down1, -1), shift(up2, 2), shift(down2, -2)
    stay, up, down = call(near_kernel, [VMEM] * 5, (keep, *parts), (one,) * 3)
    mine = call(far_kernel, [VMEM] * 3, (stay, shift(up, 4), shift(down, -4)), one)

    k9, k3, k6 = shift(mine, 3), shift(mine, -3), shift(mine, 6)
    gx = call(x_sum_kernel, [ORDER, VMEM], (mine, gx), array((NY, tokens, BS)))
    mid = call(four_kernel, [ORDER] + [VMEM] * 4, (gx, mine, k3, k6, k9), array((4, CHUNK, BS)))
    grad_x = total(swap(gx, "mp", Y_GROUPS))

    low, high = shift(mid, 1), shift(mid, -1)
    grad_w = call(
        whole_kernel,
        [SMEM, ORDER] + [VMEM] * 3,
        (rel, grad_x, mid, low, high),
        array((slots * BS, BS), F32),
        [pltpu.VMEM((NZ, CHUNK, BS), BF16)],
    )
    return grad_x, grad_w.reshape(slots, BS, BS)


def local(inputs, block_weights, block_list, grad_act):
    tokens = inputs.shape[0]
    slots = block_weights.shape[0]
    row_ids, col_ids = block_list[:, 0], block_list[:, 1]
    live = (row_ids >= 0).astype(F32)
    row = jnp.maximum(row_ids, 0)
    col = jnp.maximum(col_ids, 0)
    core = lax.axis_index("mp") % NC
    at_y, at_x, at_core = row // (NC * NX), (row // NC) % NX, row % NC
    idx = ((at_core ^ core) * NX + at_x) * NY + at_y
    out_idx = (at_x * NC + at_core) * NY + at_y
    xb = inputs.astype(BF16)
    wb = (block_weights * live[:, None, None]).astype(BF16)

    by_y = swap(jnp.broadcast_to(xb[None], (NY, tokens, BS)), "mp", Y_GROUPS)
    by_xy = swap(jnp.broadcast_to(by_y[None], (NX, NY, tokens, BS)), "mp", X_GROUPS)
    own = by_xy.reshape(HALF, tokens, BS)
    sib = lax.ppermute(own, "mp", CORE_SWAP)

    rel = (jnp.arange(NZ, dtype=jnp.int32) + NZ - lax.axis_index("dp")) % NZ
    act, gx, *parts = run_blocks(idx, out_idx, col, live, rel, own, sib, wb, grad_act)
    grad_x, grad_w = reduce_gradients(gx, *parts, rel, slots)
    return act, grad_x, grad_w


def solution(mesh):
    in_specs = (P("dp", "mp"), P("mp", None, None), P("mp", None), P("dp", "mp"))
    out_specs = (P("dp", "mp"), P("dp", "mp"), P("mp", None, None))
    return jax.shard_map(local, mesh=mesh, in_specs=in_specs, out_specs=out_specs, check_vma=False)
```

```python
import jax
import jax.numpy as jnp
from jax import lax
from jax.experimental import pallas as pl
from jax.experimental.pallas import tpu as pltpu
from jax.sharding import PartitionSpec as P

BS = 128
NY, NX, NC = 8, 4, 2
NZ = 12
HALF = NY * NX
Y_GROUPS = [[(y * NX + x) * NC + c for y in range(NY)] for x in range(NX) for c in range(NC)]
X_GROUPS = [[(y * NX + x) * NC + c for x in range(NX)] for y in range(NY) for c in range(NC)]
CORE_SWAP = [(i, i ^ 1) for i in range(HALF * NC)]
CHUNK = 416
SPLIT = 208
F32, BF16 = jnp.float32, jnp.bfloat16


def gelu_parts(pre):
    inner = 0.7978845608 * (pre + 0.044715 * pre * pre * pre)
    tanh_val = jnp.tanh(inner)
    value = 0.5 * pre * (1.0 + tanh_val)
    slope = 0.5 * (1.0 + tanh_val) + 0.5 * pre * (1.0 - tanh_val * tanh_val) * 0.7978845608 * (
        1.0 + 3.0 * 0.044715 * pre * pre
    )
    return value, slope


def dot(a, b, dims):
    return lax.dot_general(a, b, (dims, ((), ())), preferred_element_type=F32)


def block_kernel(idx_ref, out_idx_ref, col_ref, live_ref, rel_ref, own_ref, sib_ref, w_ref, g_ref,
                 act_ref, gx_out_ref, keep_ref, up1_ref, down1_ref, up2_ref, down2_ref,
                 x_ref, prod_ref, pre_ref, dpre_ref, gx_ref, gw_ref):
    slots = w_ref.shape[0]
    col_blocks = pre_ref.shape[0]
    x_ref[:HALF] = own_ref[...]
    x_ref[HALF:] = sib_ref[...]
    pre_ref[...] = jnp.zeros_like(pre_ref)
    for s in range(slots):
        prod_ref[s] = dot(x_ref[idx_ref[s]], w_ref[s], ((1,), (0,)))
    for s in range(slots):
        pre_ref[col_ref[s]] += prod_ref[s]
    for c in range(col_blocks):
        value, slope = gelu_parts(pre_ref[c])
        lanes = slice(c * BS, (c + 1) * BS)
        act_ref[:, lanes] = value
        dpre_ref[c] = (g_ref[:, lanes] * slope).astype(BF16)
    for s in range(slots):
        wgrad = dot(x_ref[idx_ref[s]], dpre_ref[col_ref[s]], ((0,), (0,)))
        wgrad = (wgrad * live_ref[s]).astype(BF16)
        done = 0
        while done < BS:
            chunk, at = divmod(s * BS + done, CHUNK)
            size = min(BS - done, CHUNK - at)
            gw_ref[rel_ref[chunk], at:at + size] = wgrad[done:done + size]
            done += size
    chunk, at = divmod(slots * BS, CHUNK)
    gw_ref[rel_ref[chunk], at:] = jnp.zeros((CHUNK - at, BS), BF16)
    for i in range(3):
        keep_ref[i] = gw_ref[4 * i]
        up1_ref[i] = gw_ref[4 * i + 1]
        down1_ref[i] = gw_ref[(4 * i + 11) % NZ]
        up2_ref[i] = gw_ref[4 * i + 2, :SPLIT]
        down2_ref[i] = gw_ref[(4 * i + 10) % NZ, SPLIT:]
    gx_ref[...] = jnp.zeros_like(gx_ref)
    for s in range(slots):
        prod_ref[s] = dot(dpre_ref[col_ref[s]], w_ref[s], ((1,), (1,)))
    for s in range(slots):
        gx_ref[out_idx_ref[s]] += prod_ref[s]
    gx_out_ref[...] = gx_ref[...].astype(BF16)


def near_kernel(keep_ref, a_ref, b_ref, c_ref, d_ref, stay_ref, up_ref, down_ref):
    for i, out in enumerate((stay_ref, up_ref, down_ref)):
        part = keep_ref[i].astype(F32) + a_ref[i].astype(F32) + b_ref[i].astype(F32)
        out[:SPLIT] = (part[:SPLIT] + c_ref[i].astype(F32)).astype(BF16)
        out[SPLIT:] = (part[SPLIT:] + d_ref[i].astype(F32)).astype(BF16)


def far_kernel(stay_ref, a_ref, b_ref, out_ref):
    out_ref[...] = (stay_ref[...].astype(F32) + a_ref[...].astype(F32) + b_ref[...].astype(F32)).astype(BF16)


def three_kernel(k0_ref, k4_ref, k8_ref, all_ref, low_ref, high_ref):
    for i, part in enumerate((k0_ref, k4_ref, k8_ref)):
        all_ref[i] = part[...]
        low_ref[i] = part[:SPLIT]
        high_ref[i] = part[SPLIT:]


def sum_kernel(after_ref, in_ref, out_ref):
    out_ref[...] = jnp.sum(in_ref[...].astype(F32), axis=0)


def whole_kernel(rel_ref, after_ref, k0_ref, k4_ref, k8_ref, low1_ref, high1_ref, low2_ref, high2_ref, out_ref, gw_ref):
    gw_ref[0] = k0_ref[...]
    gw_ref[4] = k4_ref[...]
    gw_ref[8] = k8_ref[...]
    for i in range(3):
        gw_ref[(4 * i + 11) % NZ] = low1_ref[i]
        gw_ref[4 * i + 1] = high1_ref[i]
        gw_ref[(4 * i + 10) % NZ, :SPLIT] = low2_ref[i]
        gw_ref[4 * i + 2, SPLIT:] = high2_ref[i]
    rows = out_ref.shape[0]
    for j in range(NZ):
        size = min(CHUNK, rows - j * CHUNK)
        out_ref[j * CHUNK:j * CHUNK + size] = gw_ref[rel_ref[j], :size].astype(F32)


SMEM = pl.BlockSpec(memory_space=pltpu.SMEM)
VMEM = pl.BlockSpec(memory_space=pltpu.VMEM)
ORDER = pl.BlockSpec(memory_space=pl.ANY)


def call(kernel, specs, ins, outs, scratch=(), flops=0, moved=0):
    return pl.pallas_call(
        kernel,
        out_shape=outs,
        in_specs=specs,
        out_specs=jax.tree.map(lambda _: VMEM, outs),
        scratch_shapes=scratch,
        compiler_params=pltpu.CompilerParams(vmem_limit_bytes=40 << 20),
        cost_estimate=pl.CostEstimate(flops=flops, bytes_accessed=moved, transcendentals=0),
    )(*ins)


def array(shape, kind=BF16):
    return jax.ShapeDtypeStruct(shape, kind)


def run_blocks(idx, out_idx, col, live, rel, own, sib, wb, grad_act):
    slots = wb.shape[0]
    tokens, hidden = grad_act.shape
    cols = hidden // BS
    full, half = array((3, CHUNK, BS)), array((3, SPLIT, BS))
    return call(
        block_kernel,
        [SMEM] * 5 + [VMEM] * 4,
        (idx, out_idx, col, live, rel, own, sib, wb, grad_act),
        (array((tokens, hidden), F32), array((2 * HALF, tokens, BS)), full, full, full, half, half),
        [
            pltpu.VMEM((2 * HALF, tokens, BS), BF16),
            pltpu.VMEM((slots, tokens, BS), F32),
            pltpu.VMEM((cols, tokens, BS), F32),
            pltpu.VMEM((cols, tokens, BS), BF16),
            pltpu.VMEM((2 * HALF, tokens, BS), F32),
            pltpu.VMEM((NZ, CHUNK, BS), BF16),
        ],
    )


def swap(x, axis, groups):
    return lax.all_to_all(x, axis, 0, 0, tiled=True, axis_index_groups=groups)


def shift(x, by):
    return lax.ppermute(x, "dp", [(i, (i + by) % NZ) for i in range(NZ)])


def reduce_gradients(gx, keep, up1, down1, up2, down2, rel, slots):
    tokens = gx.shape[1]
    one, full, half = array((CHUNK, BS)), array((3, CHUNK, BS)), array((3, SPLIT, BS))
    gx = swap(gx, "mp", None)
    parts = shift(up1, 1), shift(down1, -1), shift(up2, 2), shift(down2, -2)
    stay, up, down = call(near_kernel, [VMEM] * 5, (keep, *parts), (one,) * 3)
    mine = call(far_kernel, [VMEM] * 3, (stay, shift(up, 4), shift(down, -4)), one)

    k8, k4 = shift(mine, 4), shift(mine, -4)
    three, low, high = call(three_kernel, [VMEM] * 3, (mine, k4, k8), (full, half, half))
    grad_x = call(sum_kernel, [ORDER, VMEM], (three, gx), array((tokens, BS), F32))

    low1, high1, low2, high2 = shift(three, 1), shift(three, -1), shift(low, 2), shift(high, -2)
    grad_w = call(
        whole_kernel,
        [SMEM, ORDER] + [VMEM] * 7,
        (rel, grad_x, mine, k4, k8, low1, high1, low2, high2),
        array((slots * BS, BS), F32),
        [pltpu.VMEM((NZ, CHUNK, BS), BF16)],
    )
    return grad_x, grad_w.reshape(slots, BS, BS)


def local(inputs, block_weights, block_list, grad_act):
    tokens = inputs.shape[0]
    slots = block_weights.shape[0]
    row_ids, col_ids = block_list[:, 0], block_list[:, 1]
    live = (row_ids >= 0).astype(F32)
    row = jnp.maximum(row_ids, 0)
    col = jnp.maximum(col_ids, 0)
    core = lax.axis_index("mp") % NC
    at_y, at_x, at_core = row // (NC * NX), (row // NC) % NX, row % NC
    idx = ((at_core ^ core) * NX + at_x) * NY + at_y
    xb = inputs.astype(BF16)
    wb = (block_weights * live[:, None, None]).astype(BF16)

    by_y = swap(jnp.broadcast_to(xb[None], (NY, tokens, BS)), "mp", Y_GROUPS)
    by_xy = swap(jnp.broadcast_to(by_y[None], (NX, NY, tokens, BS)), "mp", X_GROUPS)
    own = by_xy.reshape(HALF, tokens, BS)
    sib = lax.ppermute(own, "mp", CORE_SWAP)

    rel = (jnp.arange(NZ, dtype=jnp.int32) + NZ - lax.axis_index("dp")) % NZ
    act, gx, *parts = run_blocks(idx, row, col, live, rel, own, sib, wb, grad_act)
    grad_x, grad_w = reduce_gradients(gx, *parts, rel, slots)
    return act, grad_x, grad_w


def solution(mesh):
    in_specs = (P("dp", "mp"), P("mp", None, None), P("mp", None), P("dp", "mp"))
    out_specs = (P("dp", "mp"), P("dp", "mp"), P("mp", None, None))
    return jax.shard_map(local, mesh=mesh, in_specs=in_specs, out_specs=out_specs, check_vma=False)
```

```python
import jax
import jax.numpy as jnp
from jax import lax
from jax.experimental import pallas as pl
from jax.experimental.pallas import tpu as pltpu
from jax.sharding import PartitionSpec as P

BS = 128
NY, NX, NC = 8, 4, 2
NZ = 12
HALF = NY * NX
Y_GROUPS = [[(y * NX + x) * NC + c for y in range(NY)] for x in range(NX) for c in range(NC)]
X_GROUPS = [[(y * NX + x) * NC + c for x in range(NX)] for y in range(NY) for c in range(NC)]
CORE_SWAP = [(i, i ^ 1) for i in range(HALF * NC)]
CHUNK = 416
Z_FAR = [[3 * i + r for i in range(4)] for r in range(3)]
F32, BF16 = jnp.float32, jnp.bfloat16


def gelu_parts(pre):
    inner = 0.7978845608 * (pre + 0.044715 * pre * pre * pre)
    tanh_val = jnp.tanh(inner)
    value = 0.5 * pre * (1.0 + tanh_val)
    slope = 0.5 * (1.0 + tanh_val) + 0.5 * pre * (1.0 - tanh_val * tanh_val) * 0.7978845608 * (
        1.0 + 3.0 * 0.044715 * pre * pre
    )
    return value, slope


def dot(a, b, dims):
    return lax.dot_general(a, b, (dims, ((), ())), preferred_element_type=F32)


def block_kernel(idx_ref, out_idx_ref, col_ref, live_ref, rel_ref, own_ref, sib_ref, w_ref, g_ref,
                 act_ref, gx_out_ref, keep_ref, up1_ref, down1_ref, up2_ref,
                 x_ref, prod_ref, pre_ref, dpre_ref, gx_ref, gw_ref):
    slots = w_ref.shape[0]
    col_blocks = pre_ref.shape[0]
    x_ref[:HALF] = own_ref[...]
    x_ref[HALF:] = sib_ref[...]
    pre_ref[...] = jnp.zeros_like(pre_ref)
    for s in range(slots):
        prod_ref[s] = dot(x_ref[idx_ref[s]], w_ref[s], ((1,), (0,)))
    for s in range(slots):
        pre_ref[col_ref[s]] += prod_ref[s]
    for c in range(col_blocks):
        value, slope = gelu_parts(pre_ref[c])
        lanes = slice(c * BS, (c + 1) * BS)
        act_ref[:, lanes] = value
        dpre_ref[c] = (g_ref[:, lanes] * slope).astype(BF16)
    for s in range(slots):
        wgrad = dot(x_ref[idx_ref[s]], dpre_ref[col_ref[s]], ((0,), (0,)))
        wgrad = (wgrad * live_ref[s]).astype(BF16)
        done = 0
        while done < BS:
            chunk, at = divmod(s * BS + done, CHUNK)
            size = min(BS - done, CHUNK - at)
            gw_ref[rel_ref[chunk], at:at + size] = wgrad[done:done + size]
            done += size
    chunk, at = divmod(slots * BS, CHUNK)
    gw_ref[rel_ref[chunk], at:] = jnp.zeros((CHUNK - at, BS), BF16)
    for i in range(3):
        keep_ref[i] = gw_ref[4 * i]
        up1_ref[i] = gw_ref[4 * i + 1]
        down1_ref[i] = gw_ref[(4 * i + 11) % NZ]
        up2_ref[i] = gw_ref[4 * i + 2]
    gx_ref[...] = jnp.zeros_like(gx_ref)
    for s in range(slots):
        prod_ref[s] = dot(dpre_ref[col_ref[s]], w_ref[s], ((1,), (1,)))
    for s in range(slots):
        gx_ref[out_idx_ref[s]] += prod_ref[s]
    gx_out_ref[...] = gx_ref[...].astype(BF16)


def near_kernel(keep_ref, a_ref, b_ref, c_ref, stay_ref, up_ref, down_ref):
    for i, out in enumerate((stay_ref, up_ref, down_ref)):
        part = keep_ref[i].astype(F32) + a_ref[i].astype(F32) + b_ref[i].astype(F32)
        out[...] = (part + c_ref[i].astype(F32)).astype(BF16)


def far_kernel(stay_ref, a_ref, b_ref, out_ref):
    out_ref[...] = (stay_ref[...].astype(F32) + a_ref[...].astype(F32) + b_ref[...].astype(F32)).astype(BF16)


def sum_kernel(after_ref, in_ref, out_ref):
    out_ref[...] = jnp.sum(in_ref[...].astype(F32), axis=0)


def whole_kernel(place_ref, after_ref, low_ref, mid_ref, high_ref, out_ref, gw_ref):
    for i, part in enumerate((low_ref, mid_ref, high_ref)):
        for b in range(4):
            gw_ref[3 * b + place_ref[i]] = part[b]
    rows = out_ref.shape[0]
    for j in range(NZ):
        size = min(CHUNK, rows - j * CHUNK)
        out_ref[j * CHUNK:j * CHUNK + size] = gw_ref[j, :size].astype(F32)


SMEM = pl.BlockSpec(memory_space=pltpu.SMEM)
VMEM = pl.BlockSpec(memory_space=pltpu.VMEM)
ORDER = pl.BlockSpec(memory_space=pl.ANY)


def call(kernel, specs, ins, outs, scratch=(), flops=0, moved=0):
    return pl.pallas_call(
        kernel,
        out_shape=outs,
        in_specs=specs,
        out_specs=jax.tree.map(lambda _: VMEM, outs),
        scratch_shapes=scratch,
        compiler_params=pltpu.CompilerParams(vmem_limit_bytes=40 << 20),
        cost_estimate=pl.CostEstimate(flops=flops, bytes_accessed=moved, transcendentals=0),
    )(*ins)


def array(shape, kind=BF16):
    return jax.ShapeDtypeStruct(shape, kind)


def run_blocks(idx, out_idx, col, live, rel, own, sib, wb, grad_act):
    slots = wb.shape[0]
    tokens, hidden = grad_act.shape
    cols = hidden // BS
    full = array((3, CHUNK, BS))
    return call(
        block_kernel,
        [SMEM] * 5 + [VMEM] * 4,
        (idx, out_idx, col, live, rel, own, sib, wb, grad_act),
        (array((tokens, hidden), F32), array((2 * HALF, tokens, BS)), full, full, full, full),
        [
            pltpu.VMEM((2 * HALF, tokens, BS), BF16),
            pltpu.VMEM((slots, tokens, BS), F32),
            pltpu.VMEM((cols, tokens, BS), F32),
            pltpu.VMEM((cols, tokens, BS), BF16),
            pltpu.VMEM((2 * HALF, tokens, BS), F32),
            pltpu.VMEM((NZ, CHUNK, BS), BF16),
        ],
    )


def swap(x, axis, groups):
    return lax.all_to_all(x, axis, 0, 0, tiled=True, axis_index_groups=groups)


def shift(x, by):
    return lax.ppermute(x, "dp", [(i, (i + by) % NZ) for i in range(NZ)])


def reduce_gradients(gx, keep, up1, down1, up2, slots):
    tokens = gx.shape[1]
    one = array((CHUNK, BS))
    gx = swap(gx, "mp", None)
    parts = shift(up1, 1), shift(down1, -1), shift(up2, 2)
    stay, up, down = call(near_kernel, [VMEM] * 4, (keep, *parts), (one,) * 3)
    mine = call(far_kernel, [VMEM] * 3, (stay, shift(up, 4), shift(down, -4)), one)

    mid = lax.all_gather(mine, "dp", axis_index_groups=Z_FAR)
    grad_x = call(sum_kernel, [ORDER, VMEM], (mid, gx), array((tokens, BS), F32))
    low, high = shift(mid, 1), shift(mid, -1)
    place = (jnp.arange(3, dtype=jnp.int32) + lax.axis_index("dp") + 2) % 3
    grad_w = call(
        whole_kernel,
        [SMEM, ORDER] + [VMEM] * 3,
        (place, grad_x, low, mid, high),
        array((slots * BS, BS), F32),
        [pltpu.VMEM((NZ, CHUNK, BS), BF16)],
    )
    return grad_x, grad_w.reshape(slots, BS, BS)


def local(inputs, block_weights, block_list, grad_act):
    tokens = inputs.shape[0]
    slots = block_weights.shape[0]
    row_ids, col_ids = block_list[:, 0], block_list[:, 1]
    live = (row_ids >= 0).astype(F32)
    row = jnp.maximum(row_ids, 0)
    col = jnp.maximum(col_ids, 0)
    core = lax.axis_index("mp") % NC
    at_y, at_x, at_core = row // (NC * NX), (row // NC) % NX, row % NC
    idx = ((at_core ^ core) * NX + at_x) * NY + at_y
    xb = inputs.astype(BF16)
    wb = (block_weights * live[:, None, None]).astype(BF16)

    by_y = swap(jnp.broadcast_to(xb[None], (NY, tokens, BS)), "mp", Y_GROUPS)
    by_xy = swap(jnp.broadcast_to(by_y[None], (NX, NY, tokens, BS)), "mp", X_GROUPS)
    own = by_xy.reshape(HALF, tokens, BS)
    sib = lax.ppermute(own, "mp", CORE_SWAP)

    rel = (jnp.arange(NZ, dtype=jnp.int32) + NZ - lax.axis_index("dp")) % NZ
    act, gx, *parts = run_blocks(idx, row, col, live, rel, own, sib, wb, grad_act)
    grad_x, grad_w = reduce_gradients(gx, *parts, slots)
    return act, grad_x, grad_w


def solution(mesh):
    in_specs = (P("dp", "mp"), P("mp", None, None), P("mp", None), P("dp", "mp"))
    out_specs = (P("dp", "mp"), P("dp", "mp"), P("mp", None, None))
    return jax.shard_map(local, mesh=mesh, in_specs=in_specs, out_specs=out_specs, check_vma=False)
```

```python
import jax
import jax.numpy as jnp
from jax import lax
from jax.experimental import pallas as pl
from jax.experimental.pallas import tpu as pltpu
from jax.sharding import PartitionSpec as P

BS = 128
NY, NX, NC = 8, 4, 2
NZ = 12
HALF = NY * NX
Y_GROUPS = [[(y * NX + x) * NC + c for y in range(NY)] for x in range(NX) for c in range(NC)]
X_GROUPS = [[(y * NX + x) * NC + c for x in range(NX)] for y in range(NY) for c in range(NC)]
CORE_SWAP = [(i, i ^ 1) for i in range(HALF * NC)]
CHUNK = 416
SPLIT = 208
Z_FAR = [[3 * i + r for i in range(4)] for r in range(3)]
F32, BF16 = jnp.float32, jnp.bfloat16


def gelu_parts(pre):
    inner = 0.7978845608 * (pre + 0.044715 * pre * pre * pre)
    tanh_val = jnp.tanh(inner)
    value = 0.5 * pre * (1.0 + tanh_val)
    slope = 0.5 * (1.0 + tanh_val) + 0.5 * pre * (1.0 - tanh_val * tanh_val) * 0.7978845608 * (
        1.0 + 3.0 * 0.044715 * pre * pre
    )
    return value, slope


def dot(a, b, dims):
    return lax.dot_general(a, b, (dims, ((), ())), preferred_element_type=F32)


def block_kernel(idx_ref, out_idx_ref, col_ref, live_ref, rel_ref, own_ref, sib_ref, w_ref, g_ref,
                 act_ref, gx_out_ref, keep_ref, up1_ref, down1_ref, up2_ref, down2_ref,
                 x_ref, prod_ref, pre_ref, dpre_ref, gx_ref, gw_ref, x_out_ref, sem):
    slots = w_ref.shape[0]
    col_blocks = pre_ref.shape[0]
    x_ref[:HALF] = own_ref[...]
    x_ref[HALF:] = sib_ref[...]
    pre_ref[...] = jnp.zeros_like(pre_ref)
    for s in range(slots):
        prod_ref[s] = dot(x_ref[idx_ref[s]], w_ref[s], ((1,), (0,)))
    for s in range(slots):
        pre_ref[col_ref[s]] += prod_ref[s]
    for c in range(col_blocks):
        value, slope = gelu_parts(pre_ref[c])
        lanes = slice(c * BS, (c + 1) * BS)
        act_ref[:, lanes] = value
        dpre_ref[c] = (g_ref[:, lanes] * slope).astype(BF16)
    gx_ref[...] = jnp.zeros_like(gx_ref)
    for s in range(slots):
        prod_ref[s] = dot(dpre_ref[col_ref[s]], w_ref[s], ((1,), (1,)))
    for s in range(slots):
        gx_ref[out_idx_ref[s]] += prod_ref[s]
    x_out_ref[...] = gx_ref[...].astype(BF16)
    copy = pltpu.make_async_copy(x_out_ref, gx_out_ref, sem)
    copy.start()
    for s in range(slots):
        wgrad = dot(x_ref[idx_ref[s]], dpre_ref[col_ref[s]], ((0,), (0,)))
        wgrad = (wgrad * live_ref[s]).astype(BF16)
        done = 0
        while done < BS:
            chunk, at = divmod(s * BS + done, CHUNK)
            size = min(BS - done, CHUNK - at)
            gw_ref[rel_ref[chunk], at:at + size] = wgrad[done:done + size]
            done += size
    chunk, at = divmod(slots * BS, CHUNK)
    gw_ref[rel_ref[chunk], at:] = jnp.zeros((CHUNK - at, BS), BF16)
    for i in range(3):
        keep_ref[i] = gw_ref[4 * i]
        up1_ref[i] = gw_ref[4 * i + 1]
        down1_ref[i] = gw_ref[(4 * i + 11) % NZ]
        up2_ref[i] = gw_ref[4 * i + 2, :SPLIT]
        down2_ref[i] = gw_ref[(4 * i + 10) % NZ, SPLIT:]
    copy.wait()


def near_kernel(keep_ref, a_ref, b_ref, c_ref, d_ref, stay_ref, up_ref, down_ref):
    for i, out in enumerate((stay_ref, up_ref, down_ref)):
        part = keep_ref[i].astype(F32) + a_ref[i].astype(F32) + b_ref[i].astype(F32)
        out[:SPLIT] = (part[:SPLIT] + c_ref[i].astype(F32)).astype(BF16)
        out[SPLIT:] = (part[SPLIT:] + d_ref[i].astype(F32)).astype(BF16)


def far_kernel(stay_ref, a_ref, b_ref, out_ref):
    out_ref[...] = (stay_ref[...].astype(F32) + a_ref[...].astype(F32) + b_ref[...].astype(F32)).astype(BF16)


def sum_kernel(after_ref, in_ref, out_ref):
    out_ref[...] = jnp.sum(in_ref[...].astype(F32), axis=0)


def whole_kernel(place_ref, after_ref, low_ref, mid_ref, high_ref, out_ref, gw_ref):
    for i, part in enumerate((low_ref, mid_ref, high_ref)):
        for b in range(4):
            gw_ref[3 * b + place_ref[i]] = part[b]
    rows = out_ref.shape[0]
    for j in range(NZ):
        size = min(CHUNK, rows - j * CHUNK)
        out_ref[j * CHUNK:j * CHUNK + size] = gw_ref[j, :size].astype(F32)


SMEM = pl.BlockSpec(memory_space=pltpu.SMEM)
VMEM = pl.BlockSpec(memory_space=pltpu.VMEM)
ORDER = pl.BlockSpec(memory_space=pl.ANY)


def call(kernel, specs, ins, outs, scratch=(), out_specs=None):
    return pl.pallas_call(
        kernel,
        out_shape=outs,
        in_specs=specs,
        out_specs=out_specs or jax.tree.map(lambda _: VMEM, outs),
        scratch_shapes=scratch,
        compiler_params=pltpu.CompilerParams(vmem_limit_bytes=40 << 20),
    )(*ins)


def array(shape, kind=BF16):
    return jax.ShapeDtypeStruct(shape, kind)


def run_blocks(idx, out_idx, col, live, rel, own, sib, wb, grad_act):
    slots = wb.shape[0]
    tokens, hidden = grad_act.shape
    cols = hidden // BS
    full, half = array((3, CHUNK, BS)), array((3, SPLIT, BS))
    return call(
        block_kernel,
        [SMEM] * 5 + [VMEM] * 4,
        (idx, out_idx, col, live, rel, own, sib, wb, grad_act),
        (array((tokens, hidden), F32), pltpu.HBM((2 * HALF, tokens, BS), BF16), full, full, full, half, half),
        [
            pltpu.VMEM((2 * HALF, tokens, BS), BF16),
            pltpu.VMEM((slots, tokens, BS), F32),
            pltpu.VMEM((cols, tokens, BS), F32),
            pltpu.VMEM((cols, tokens, BS), BF16),
            pltpu.VMEM((2 * HALF, tokens, BS), F32),
            pltpu.VMEM((NZ, CHUNK, BS), BF16),
            pltpu.VMEM((2 * HALF, tokens, BS), BF16),
            pltpu.SemaphoreType.DMA,
        ],
        (VMEM, pl.BlockSpec(memory_space=pltpu.HBM)) + (VMEM,) * 5,
    )


def swap(x, axis, groups):
    return lax.all_to_all(x, axis, 0, 0, tiled=True, axis_index_groups=groups)


def shift(x, by):
    return lax.ppermute(x, "dp", [(i, (i + by) % NZ) for i in range(NZ)])


def reduce_gradients(gx, keep, up1, down1, up2, down2, slots):
    tokens = gx.shape[1]
    one = array((CHUNK, BS))
    gx = swap(gx, "mp", None)
    parts = shift(up1, 1), shift(down1, -1), shift(up2, 2), shift(down2, -2)
    stay, up, down = call(near_kernel, [VMEM] * 5, (keep, *parts), (one,) * 3)
    mine = call(far_kernel, [VMEM] * 3, (stay, shift(up, 4), shift(down, -4)), one)

    mid = lax.all_gather(mine, "dp", axis_index_groups=Z_FAR)
    grad_x = call(sum_kernel, [ORDER, VMEM], (mid, gx), array((tokens, BS), F32))
    low, high = shift(mid, 1), shift(mid, -1)
    place = (jnp.arange(3, dtype=jnp.int32) + lax.axis_index("dp") + 2) % 3
    grad_w = call(
        whole_kernel,
        [SMEM, ORDER] + [VMEM] * 3,
        (place, grad_x, low, mid, high),
        array((slots * BS, BS), F32),
        [pltpu.VMEM((NZ, CHUNK, BS), BF16)],
    )
    return grad_x, grad_w.reshape(slots, BS, BS)


def local(inputs, block_weights, block_list, grad_act):
    tokens = inputs.shape[0]
    slots = block_weights.shape[0]
    row_ids, col_ids = block_list[:, 0], block_list[:, 1]
    live = (row_ids >= 0).astype(F32)
    row = jnp.maximum(row_ids, 0)
    col = jnp.maximum(col_ids, 0)
    core = lax.axis_index("mp") % NC
    at_y, at_x, at_core = row // (NC * NX), (row // NC) % NX, row % NC
    idx = ((at_core ^ core) * NX + at_x) * NY + at_y
    xb = inputs.astype(BF16)
    wb = (block_weights * live[:, None, None]).astype(BF16)

    by_y = swap(jnp.broadcast_to(xb[None], (NY, tokens, BS)), "mp", Y_GROUPS)
    by_xy = swap(jnp.broadcast_to(by_y[None], (NX, NY, tokens, BS)), "mp", X_GROUPS)
    own = by_xy.reshape(HALF, tokens, BS)
    sib = lax.ppermute(own, "mp", CORE_SWAP)

    rel = (jnp.arange(NZ, dtype=jnp.int32) + NZ - lax.axis_index("dp")) % NZ
    act, gx, *parts = run_blocks(idx, row, col, live, rel, own, sib, wb, grad_act)
    grad_x, grad_w = reduce_gradients(gx, *parts, slots)
    return act, grad_x, grad_w


def solution(mesh):
    in_specs = (P("dp", "mp"), P("mp", None, None), P("mp", None), P("dp", "mp"))
    out_specs = (P("dp", "mp"), P("dp", "mp"), P("mp", None, None))
    return jax.shard_map(local, mesh=mesh, in_specs=in_specs, out_specs=out_specs, check_vma=False)
```

```python
import jax
import jax.numpy as jnp
from jax import lax
from jax.experimental import pallas as pl
from jax.experimental.pallas import tpu as pltpu
from jax.sharding import PartitionSpec as P

BS = 128
NY, NX, NC = 8, 4, 2
NZ = 12
HALF = NY * NX
Y_GROUPS = [[(y * NX + x) * NC + c for y in range(NY)] for x in range(NX) for c in range(NC)]
X_GROUPS = [[(y * NX + x) * NC + c for x in range(NX)] for y in range(NY) for c in range(NC)]
CORE_SWAP = [(i, i ^ 1) for i in range(HALF * NC)]
CHUNK = 416
SPLIT = 208
PIECES = 4
Z_FAR = [[3 * i + r for i in range(4)] for r in range(3)]
F32, BF16 = jnp.float32, jnp.bfloat16


def gelu_parts(pre):
    inner = 0.7978845608 * (pre + 0.044715 * pre * pre * pre)
    tanh_val = jnp.tanh(inner)
    value = 0.5 * pre * (1.0 + tanh_val)
    slope = 0.5 * (1.0 + tanh_val) + 0.5 * pre * (1.0 - tanh_val * tanh_val) * 0.7978845608 * (
        1.0 + 3.0 * 0.044715 * pre * pre
    )
    return value, slope


def dot(a, b, dims):
    return lax.dot_general(a, b, (dims, ((), ())), preferred_element_type=F32)


def block_kernel(idx_ref, out_idx_ref, col_ref, live_ref, rel_ref, own_ref, sib_ref, w_ref, g_ref,
                 act_ref, gx_out_ref, keep_ref, up1_ref, down1_ref, up2_ref, down2_ref,
                 x_ref, prod_ref, pre_ref, dpre_ref, gx_ref, gw_ref, x_out_ref, sems):
    slots = w_ref.shape[0]
    col_blocks = pre_ref.shape[0]
    x_ref[:HALF] = own_ref[...]
    x_ref[HALF:] = sib_ref[...]
    pre_ref[...] = jnp.zeros_like(pre_ref)
    for s in range(slots):
        prod_ref[s] = dot(x_ref[idx_ref[s]], w_ref[s], ((1,), (0,)))
    for s in range(slots):
        pre_ref[col_ref[s]] += prod_ref[s]
    for c in range(col_blocks):
        value, slope = gelu_parts(pre_ref[c])
        lanes = slice(c * BS, (c + 1) * BS)
        act_ref[:, lanes] = value
        dpre_ref[c] = (g_ref[:, lanes] * slope).astype(BF16)
    for s in range(slots):
        wgrad = dot(x_ref[idx_ref[s]], dpre_ref[col_ref[s]], ((0,), (0,)))
        wgrad = (wgrad * live_ref[s]).astype(BF16)
        done = 0
        while done < BS:
            chunk, at = divmod(s * BS + done, CHUNK)
            size = min(BS - done, CHUNK - at)
            gw_ref[rel_ref[chunk], at:at + size] = wgrad[done:done + size]
            done += size
    chunk, at = divmod(slots * BS, CHUNK)
    gw_ref[rel_ref[chunk], at:] = jnp.zeros((CHUNK - at, BS), BF16)
    for i in range(3):
        keep_ref[i] = gw_ref[4 * i]
        up1_ref[i] = gw_ref[4 * i + 1]
        down1_ref[i] = gw_ref[(4 * i + 11) % NZ]
        up2_ref[i] = gw_ref[4 * i + 2, :SPLIT]
        down2_ref[i] = gw_ref[(4 * i + 10) % NZ, SPLIT:]
    gx_ref[...] = jnp.zeros_like(gx_ref)
    for s in range(slots):
        prod_ref[s] = dot(dpre_ref[col_ref[s]], w_ref[s], ((1,), (1,)))
    for s in range(slots):
        gx_ref[out_idx_ref[s]] += prod_ref[s]
    copies = []
    size = gx_ref.shape[0] // PIECES
    for p in range(PIECES):
        part = pl.ds(p * size, size)
        x_out_ref[part] = gx_ref[part].astype(BF16)
        copies.append(pltpu.make_async_copy(x_out_ref.at[part], gx_out_ref.at[part], sems.at[p]))
        copies[-1].start()
    for copy in copies:
        copy.wait()


def near_kernel(keep_ref, a_ref, b_ref, c_ref, d_ref, stay_ref, up_ref, down_ref):
    for i, out in enumerate((stay_ref, up_ref, down_ref)):
        part = keep_ref[i].astype(F32) + a_ref[i].astype(F32) + b_ref[i].astype(F32)
        out[:SPLIT] = (part[:SPLIT] + c_ref[i].astype(F32)).astype(BF16)
        out[SPLIT:] = (part[SPLIT:] + d_ref[i].astype(F32)).astype(BF16)


def far_kernel(stay_ref, a_ref, b_ref, out_ref):
    out_ref[...] = (stay_ref[...].astype(F32) + a_ref[...].astype(F32) + b_ref[...].astype(F32)).astype(BF16)


def sum_kernel(after_ref, in_ref, out_ref):
    out_ref[...] = jnp.sum(in_ref[...].astype(F32), axis=0)


def whole_kernel(place_ref, after_ref, low_ref, mid_ref, high_ref, out_ref, gw_ref, wide_ref, sems):
    for i, part in enumerate((low_ref, mid_ref, high_ref)):
        for b in range(4):
            gw_ref[3 * b + place_ref[i]] = part[b]
    rows = out_ref.shape[0]
    copies = []
    for j in range(NZ):
        size = min(CHUNK, rows - j * CHUNK)
        wide_ref[j, :size] = gw_ref[j, :size].astype(F32)
        copies.append(
            pltpu.make_async_copy(
                wide_ref.at[j, pl.ds(0, size)], out_ref.at[pl.ds(j * CHUNK, size)], sems.at[j]
            )
        )
        copies[-1].start()
    for copy in copies:
        copy.wait()


def first_spread_kernel(in_ref, out_ref):
    value = in_ref[...].astype(BF16)
    for i in range(out_ref.shape[0]):
        out_ref[i] = value


def second_spread_kernel(in_ref, out_ref, sems):
    copies = [
        pltpu.make_async_copy(in_ref, out_ref.at[i], sems.at[i]) for i in range(out_ref.shape[0])
    ]
    for copy in copies:
        copy.start()
    for copy in copies:
        copy.wait()


SMEM = pl.BlockSpec(memory_space=pltpu.SMEM)
VMEM = pl.BlockSpec(memory_space=pltpu.VMEM)
HBM = pl.BlockSpec(memory_space=pltpu.HBM)
ORDER = pl.BlockSpec(memory_space=pl.ANY)


def call(kernel, specs, ins, outs, scratch=(), out_specs=None):
    return pl.pallas_call(
        kernel,
        out_shape=outs,
        in_specs=specs,
        out_specs=out_specs or jax.tree.map(lambda _: VMEM, outs),
        scratch_shapes=scratch,
        compiler_params=pltpu.CompilerParams(vmem_limit_bytes=40 << 20),
    )(*ins)


def array(shape, kind=BF16):
    return jax.ShapeDtypeStruct(shape, kind)


def run_blocks(idx, out_idx, col, live, rel, own, sib, wb, grad_act):
    slots = wb.shape[0]
    tokens, hidden = grad_act.shape
    cols = hidden // BS
    full, half = array((3, CHUNK, BS)), array((3, SPLIT, BS))
    return call(
        block_kernel,
        [SMEM] * 5 + [VMEM] * 4,
        (idx, out_idx, col, live, rel, own, sib, wb, grad_act),
        (array((tokens, hidden), F32), pltpu.HBM((2 * HALF, tokens, BS), BF16), full, full, full, half, half),
        [
            pltpu.VMEM((2 * HALF, tokens, BS), BF16),
            pltpu.VMEM((slots, tokens, BS), F32),
            pltpu.VMEM((cols, tokens, BS), F32),
            pltpu.VMEM((cols, tokens, BS), BF16),
            pltpu.VMEM((2 * HALF, tokens, BS), F32),
            pltpu.VMEM((NZ, CHUNK, BS), BF16),
            pltpu.VMEM((2 * HALF, tokens, BS), BF16),
            pltpu.SemaphoreType.DMA((PIECES,)),
        ],
        (VMEM, HBM) + (VMEM,) * 5,
    )


def swap(x, axis, groups):
    return lax.all_to_all(x, axis, 0, 0, tiled=True, axis_index_groups=groups)


def shift(x, by):
    return lax.ppermute(x, "dp", [(i, (i + by) % NZ) for i in range(NZ)])


def reduce_gradients(gx, keep, up1, down1, up2, down2, slots):
    tokens = gx.shape[1]
    one = array((CHUNK, BS))
    gx = swap(gx, "mp", None)
    parts = shift(up1, 1), shift(down1, -1), shift(up2, 2), shift(down2, -2)
    stay, up, down = call(near_kernel, [VMEM] * 5, (keep, *parts), (one,) * 3)
    mine = call(far_kernel, [VMEM] * 3, (stay, shift(up, 4), shift(down, -4)), one)

    mid = lax.all_gather(mine, "dp", axis_index_groups=Z_FAR)
    grad_x = call(sum_kernel, [ORDER, VMEM], (mid, gx), array((tokens, BS), F32))
    low, high = shift(mid, 1), shift(mid, -1)
    place = (jnp.arange(3, dtype=jnp.int32) + lax.axis_index("dp") + 2) % 3
    grad_w = call(
        whole_kernel,
        [SMEM, ORDER] + [VMEM] * 3,
        (place, grad_x, low, mid, high),
        pltpu.HBM((slots * BS, BS), F32),
        [
            pltpu.VMEM((NZ, CHUNK, BS), BF16),
            pltpu.VMEM((NZ, CHUNK, BS), F32),
            pltpu.SemaphoreType.DMA((NZ,)),
        ],
        HBM,
    )
    return grad_x, grad_w.reshape(slots, BS, BS)


def local(inputs, block_weights, block_list, grad_act):
    tokens = inputs.shape[0]
    slots = block_weights.shape[0]
    row_ids, col_ids = block_list[:, 0], block_list[:, 1]
    live = (row_ids >= 0).astype(F32)
    row = jnp.maximum(row_ids, 0)
    col = jnp.maximum(col_ids, 0)
    core = lax.axis_index("mp") % NC
    at_y, at_x, at_core = row // (NC * NX), (row // NC) % NX, row % NC
    idx = ((at_core ^ core) * NX + at_x) * NY + at_y
    wb = (block_weights * live[:, None, None]).astype(BF16)

    by_y = call(first_spread_kernel, [VMEM], (inputs,), array((NY, tokens, BS)))
    by_y = swap(by_y, "mp", Y_GROUPS)
    by_xy = call(
        second_spread_kernel,
        [VMEM],
        (by_y,),
        pltpu.HBM((NX, NY, tokens, BS), BF16),
        [pltpu.SemaphoreType.DMA((NX,))],
        HBM,
    )
    by_xy = swap(by_xy, "mp", X_GROUPS)
    own = by_xy.reshape(HALF, tokens, BS)
    sib = lax.ppermute(own, "mp", CORE_SWAP)

    rel = (jnp.arange(NZ, dtype=jnp.int32) + NZ - lax.axis_index("dp")) % NZ
    act, gx, *parts = run_blocks(idx, row, col, live, rel, own, sib, wb, grad_act)
    grad_x, grad_w = reduce_gradients(gx, *parts, slots)
    return act, grad_x, grad_w


def solution(mesh):
    in_specs = (P("dp", "mp"), P("mp", None, None), P("mp", None), P("dp", "mp"))
    out_specs = (P("dp", "mp"), P("dp", "mp"), P("mp", None, None))
    return jax.shard_map(local, mesh=mesh, in_specs=in_specs, out_specs=out_specs, check_vma=False)
```

```python
import jax
import jax.numpy as jnp
from jax import lax
from jax.experimental import pallas as pl
from jax.experimental.pallas import tpu as pltpu
from jax.sharding import PartitionSpec as P

BS = 128
NY, NX, NC = 8, 4, 2
NZ = 12
HALF = NY * NX
Y_GROUPS = [[(y * NX + x) * NC + c for y in range(NY)] for x in range(NX) for c in range(NC)]
X_GROUPS = [[(y * NX + x) * NC + c for x in range(NX)] for y in range(NY) for c in range(NC)]
CORE_SWAP = [(i, i ^ 1) for i in range(HALF * NC)]
CHUNK = 416
SPLIT = 208
PIECES = 4
Z_EVEN_ODD = [[2 * i + r for i in range(6)] for r in range(2)]
F32, BF16 = jnp.float32, jnp.bfloat16


def gelu_parts(pre):
    inner = 0.7978845608 * (pre + 0.044715 * pre * pre * pre)
    tanh_val = jnp.tanh(inner)
    value = 0.5 * pre * (1.0 + tanh_val)
    slope = 0.5 * (1.0 + tanh_val) + 0.5 * pre * (1.0 - tanh_val * tanh_val) * 0.7978845608 * (
        1.0 + 3.0 * 0.044715 * pre * pre
    )
    return value, slope


def dot(a, b, dims):
    return lax.dot_general(a, b, (dims, ((), ())), preferred_element_type=F32)


def block_kernel(idx_ref, out_idx_ref, col_ref, live_ref, rel_ref, own_ref, sib_ref, w_ref, g_ref,
                 act_ref, gx_out_ref, keep_ref, up1_ref, down1_ref, up2_ref, down2_ref,
                 x_ref, prod_ref, pre_ref, dpre_ref, gx_ref, gw_ref, x_out_ref, sems):
    slots = w_ref.shape[0]
    col_blocks = pre_ref.shape[0]
    x_ref[:HALF] = own_ref[...]
    x_ref[HALF:] = sib_ref[...]
    pre_ref[...] = jnp.zeros_like(pre_ref)
    for s in range(slots):
        prod_ref[s] = dot(x_ref[idx_ref[s]], w_ref[s], ((1,), (0,)))
    for s in range(slots):
        pre_ref[col_ref[s]] += prod_ref[s]
    for c in range(col_blocks):
        value, slope = gelu_parts(pre_ref[c])
        lanes = slice(c * BS, (c + 1) * BS)
        act_ref[:, lanes] = value
        dpre_ref[c] = (g_ref[:, lanes] * slope).astype(BF16)
    for s in range(slots):
        wgrad = dot(x_ref[idx_ref[s]], dpre_ref[col_ref[s]], ((0,), (0,)))
        wgrad = (wgrad * live_ref[s]).astype(BF16)
        done = 0
        while done < BS:
            chunk, at = divmod(s * BS + done, CHUNK)
            size = min(BS - done, CHUNK - at)
            gw_ref[rel_ref[chunk], at:at + size] = wgrad[done:done + size]
            done += size
    chunk, at = divmod(slots * BS, CHUNK)
    gw_ref[rel_ref[chunk], at:] = jnp.zeros((CHUNK - at, BS), BF16)
    for i in range(3):
        keep_ref[i] = gw_ref[4 * i]
        up1_ref[i] = gw_ref[4 * i + 1]
        down1_ref[i] = gw_ref[(4 * i + 11) % NZ]
        up2_ref[i] = gw_ref[4 * i + 2, :SPLIT]
        down2_ref[i] = gw_ref[(4 * i + 10) % NZ, SPLIT:]
    gx_ref[...] = jnp.zeros_like(gx_ref)
    for s in range(slots):
        prod_ref[s] = dot(dpre_ref[col_ref[s]], w_ref[s], ((1,), (1,)))
    for s in range(slots):
        gx_ref[out_idx_ref[s]] += prod_ref[s]
    copies = []
    size = gx_ref.shape[0] // PIECES
    for p in range(PIECES):
        part = pl.ds(p * size, size)
        x_out_ref[part] = gx_ref[part].astype(BF16)
        copies.append(pltpu.make_async_copy(x_out_ref.at[part], gx_out_ref.at[part], sems.at[p]))
        copies[-1].start()
    for copy in copies:
        copy.wait()


def near_kernel(keep_ref, a_ref, b_ref, c_ref, d_ref, stay_ref, up_ref, down_ref):
    for i, out in enumerate((stay_ref, up_ref, down_ref)):
        part = keep_ref[i].astype(F32) + a_ref[i].astype(F32) + b_ref[i].astype(F32)
        out[:SPLIT] = (part[:SPLIT] + c_ref[i].astype(F32)).astype(BF16)
        out[SPLIT:] = (part[SPLIT:] + d_ref[i].astype(F32)).astype(BF16)


def far_kernel(stay_ref, a_ref, b_ref, out_ref):
    out_ref[...] = (stay_ref[...].astype(F32) + a_ref[...].astype(F32) + b_ref[...].astype(F32)).astype(BF16)


def sum_kernel(after_ref, in_ref, out_ref, token_ref):
    out_ref[...] = jnp.sum(in_ref[...].astype(F32), axis=0)
    token_ref[...] = jnp.zeros_like(token_ref)


def halve_kernel(in_ref, low_ref, high_ref):
    low_ref[...] = in_ref[:3]
    high_ref[...] = in_ref[3:]


def write_chunks(first, parts, out_ref, wide_ref, sems):
    rows = out_ref.shape[0]
    for i, part in enumerate(parts):
        wide_ref[i] = part.astype(F32)
    for parity in range(2):

        @pl.when(first == parity)
        def write():
            copies = []
            for i in range(len(parts)):
                at = (2 * i + parity) * CHUNK
                size = min(CHUNK, rows - at)
                copies.append(
                    pltpu.make_async_copy(
                        wide_ref.at[i, pl.ds(0, size)], out_ref.at[pl.ds(at, size)], sems.at[i]
                    )
                )
                copies[-1].start()
            for copy in copies:
                copy.wait()


def own_parity_kernel(first_ref, token_ref, mid_ref, out_ref, wide_ref, sems):
    write_chunks(first_ref[0], [mid_ref[i] for i in range(6)], out_ref, wide_ref, sems)


def other_parity_kernel(first_ref, done_ref, low_ref, high_ref, out_ref, wide_ref, sems):
    parts = [low_ref[i] for i in range(3)] + [high_ref[i] for i in range(3)]
    write_chunks(1 - first_ref[0], parts, out_ref, wide_ref, sems)


def first_spread_kernel(in_ref, out_ref):
    value = in_ref[...].astype(BF16)
    for i in range(out_ref.shape[0]):
        out_ref[i] = value


def second_spread_kernel(in_ref, out_ref, sems):
    copies = [
        pltpu.make_async_copy(in_ref, out_ref.at[i], sems.at[i]) for i in range(out_ref.shape[0])
    ]
    for copy in copies:
        copy.start()
    for copy in copies:
        copy.wait()


SMEM = pl.BlockSpec(memory_space=pltpu.SMEM)
VMEM = pl.BlockSpec(memory_space=pltpu.VMEM)
HBM = pl.BlockSpec(memory_space=pltpu.HBM)
ORDER = pl.BlockSpec(memory_space=pl.ANY)


def call(kernel, specs, ins, outs, scratch=(), out_specs=None, aliases=None):
    return pl.pallas_call(
        kernel,
        out_shape=outs,
        in_specs=specs,
        out_specs=out_specs or jax.tree.map(lambda _: VMEM, outs),
        scratch_shapes=scratch,
        input_output_aliases=aliases or {},
        compiler_params=pltpu.CompilerParams(vmem_limit_bytes=20 << 20),
    )(*ins)


def array(shape, kind=BF16):
    return jax.ShapeDtypeStruct(shape, kind)


def run_blocks(idx, out_idx, col, live, rel, own, sib, wb, grad_act):
    slots = wb.shape[0]
    tokens, hidden = grad_act.shape
    cols = hidden // BS
    full, half = pltpu.VMEM((3, CHUNK, BS), BF16), pltpu.VMEM((3, SPLIT, BS), BF16)
    return call(
        block_kernel,
        [SMEM] * 5 + [VMEM] * 4,
        (idx, out_idx, col, live, rel, own, sib, wb, grad_act),
        (array((tokens, hidden), F32), pltpu.HBM((2 * HALF, tokens, BS), BF16), full, full, full, half, half),
        [
            pltpu.VMEM((2 * HALF, tokens, BS), BF16),
            pltpu.VMEM((slots, tokens, BS), F32),
            pltpu.VMEM((cols, tokens, BS), F32),
            pltpu.VMEM((cols, tokens, BS), BF16),
            pltpu.VMEM((2 * HALF, tokens, BS), F32),
            pltpu.VMEM((NZ, CHUNK, BS), BF16),
            pltpu.VMEM((2 * HALF, tokens, BS), BF16),
            pltpu.SemaphoreType.DMA((PIECES,)),
        ],
        (VMEM, HBM) + (VMEM,) * 5,
    )


def swap(x, axis, groups):
    return lax.all_to_all(x, axis, 0, 0, tiled=True, axis_index_groups=groups)


def shift(x, by):
    return lax.ppermute(x, "dp", [(i, (i + by) % NZ) for i in range(NZ)])


def reduce_gradients(gx, keep, up1, down1, up2, down2, slots):
    tokens = gx.shape[1]
    one = array((CHUNK, BS))
    gx = swap(gx, "mp", None)
    parts = shift(up1, 1), shift(down1, -1), shift(up2, 2), shift(down2, -2)
    stay, up, down = call(near_kernel, [VMEM] * 5, (keep, *parts), (one,) * 3)
    mine = call(far_kernel, [VMEM] * 3, (stay, shift(up, 4), shift(down, -4)), one)

    mid = lax.all_gather(mine, "dp", axis_index_groups=Z_EVEN_ODD)
    full = pltpu.VMEM((3, CHUNK, BS), BF16)
    low, high = call(halve_kernel, [VMEM], (mid,), (full, full))
    low, high = shift(low, 1), shift(high, -1)
    grad_x, token = call(
        sum_kernel, [ORDER, VMEM], (mid, gx), (array((tokens, BS), F32), array((8, BS), F32))
    )
    first = (lax.axis_index("dp") % 2).astype(jnp.int32).reshape(1)
    scratch = [pltpu.VMEM((6, CHUNK, BS), F32), pltpu.SemaphoreType.DMA((6,))]
    result = pltpu.HBM((slots * BS, BS), F32)
    grad_w = call(own_parity_kernel, [SMEM, VMEM, VMEM], (first, token, mid), result, scratch, HBM)
    grad_w = call(
        other_parity_kernel,
        [SMEM, HBM, VMEM, VMEM],
        (first, grad_w, low, high),
        result,
        scratch,
        HBM,
        {1: 0},
    )
    return grad_x, grad_w.reshape(slots, BS, BS)


def local(inputs, block_weights, block_list, grad_act):
    tokens = inputs.shape[0]
    slots = block_weights.shape[0]
    row_ids, col_ids = block_list[:, 0], block_list[:, 1]
    live = (row_ids >= 0).astype(F32)
    row = jnp.maximum(row_ids, 0)
    col = jnp.maximum(col_ids, 0)
    core = lax.axis_index("mp") % NC
    at_y, at_x, at_core = row // (NC * NX), (row // NC) % NX, row % NC
    idx = ((at_core ^ core) * NX + at_x) * NY + at_y
    wb = (block_weights * live[:, None, None]).astype(BF16)

    by_y = call(first_spread_kernel, [VMEM], (inputs,), array((NY, tokens, BS)))
    by_y = swap(by_y, "mp", Y_GROUPS)
    by_xy = call(
        second_spread_kernel,
        [VMEM],
        (by_y,),
        pltpu.HBM((NX, NY, tokens, BS), BF16),
        [pltpu.SemaphoreType.DMA((NX,))],
        HBM,
    )
    by_xy = swap(by_xy, "mp", X_GROUPS)
    own = by_xy.reshape(HALF, tokens, BS)
    sib = lax.ppermute(own, "mp", CORE_SWAP)

    rel = (jnp.arange(NZ, dtype=jnp.int32) + NZ - lax.axis_index("dp")) % NZ
    act, gx, *parts = run_blocks(idx, row, col, live, rel, own, sib, wb, grad_act)
    grad_x, grad_w = reduce_gradients(gx, *parts, slots)
    return act, grad_x, grad_w


def solution(mesh):
    in_specs = (P("dp", "mp"), P("mp", None, None), P("mp", None), P("dp", "mp"))
    out_specs = (P("dp", "mp"), P("dp", "mp"), P("mp", None, None))
    return jax.shard_map(local, mesh=mesh, in_specs=in_specs, out_specs=out_specs, check_vma=False)
```

```python
import jax
import jax.numpy as jnp
from jax import lax
from jax.experimental import pallas as pl
from jax.experimental.pallas import tpu as pltpu
from jax.sharding import PartitionSpec as P

BS = 128
NY, NX, NC = 8, 4, 2
NZ = 12
HALF = NY * NX
Y_GROUPS = [[(y * NX + x) * NC + c for y in range(NY)] for x in range(NX) for c in range(NC)]
X_GROUPS = [[(y * NX + x) * NC + c for x in range(NX)] for y in range(NY) for c in range(NC)]
CORE_SWAP = [(i, i ^ 1) for i in range(HALF * NC)]
CHUNK = 416
SPLIT = 208
PIECES = 4
Z_FAR = [[3 * i + r for i in range(4)] for r in range(3)]
F32, BF16 = jnp.float32, jnp.bfloat16


def gelu_parts(pre):
    inner = 0.7978845608 * (pre + 0.044715 * pre * pre * pre)
    tanh_val = jnp.tanh(inner)
    value = 0.5 * pre * (1.0 + tanh_val)
    slope = 0.5 * (1.0 + tanh_val) + 0.5 * pre * (1.0 - tanh_val * tanh_val) * 0.7978845608 * (
        1.0 + 3.0 * 0.044715 * pre * pre
    )
    return value, slope


def dot(a, b, dims):
    return lax.dot_general(a, b, (dims, ((), ())), preferred_element_type=F32)


def block_kernel(idx_ref, out_idx_ref, col_ref, live_ref, rel_ref, own_ref, sib_ref, w_ref, g_ref,
                 act_ref, gx_out_ref, keep_ref, up1_ref, down1_ref, up2_ref, down2_ref,
                 x_ref, prod_ref, pre_ref, dpre_ref, gx_ref, gw_ref, x_out_ref, sems):
    slots = w_ref.shape[0]
    col_blocks = pre_ref.shape[0]
    x_ref[:HALF] = own_ref[...]
    x_ref[HALF:] = sib_ref[...]
    pre_ref[...] = jnp.zeros_like(pre_ref)
    for s in range(slots):
        prod_ref[s] = dot(x_ref[idx_ref[s]], w_ref[s], ((1,), (0,)))
    for s in range(slots):
        pre_ref[col_ref[s]] += prod_ref[s]
    for c in range(col_blocks):
        value, slope = gelu_parts(pre_ref[c])
        lanes = slice(c * BS, (c + 1) * BS)
        act_ref[:, lanes] = value
        dpre_ref[c] = (g_ref[:, lanes] * slope).astype(BF16)
    for s in range(slots):
        wgrad = dot(x_ref[idx_ref[s]], dpre_ref[col_ref[s]], ((0,), (0,)))
        wgrad = (wgrad * live_ref[s]).astype(BF16)
        done = 0
        while done < BS:
            chunk, at = divmod(s * BS + done, CHUNK)
            size = min(BS - done, CHUNK - at)
            gw_ref[rel_ref[chunk], at:at + size] = wgrad[done:done + size]
            done += size
    chunk, at = divmod(slots * BS, CHUNK)
    gw_ref[rel_ref[chunk], at:] = jnp.zeros((CHUNK - at, BS), BF16)
    for i in range(3):
        keep_ref[i] = gw_ref[4 * i]
        up1_ref[i] = gw_ref[4 * i + 1]
        down1_ref[i] = gw_ref[(4 * i + 11) % NZ]
        up2_ref[i] = gw_ref[4 * i + 2, :SPLIT]
        down2_ref[i] = gw_ref[(4 * i + 10) % NZ, SPLIT:]
    gx_ref[...] = jnp.zeros_like(gx_ref)
    for s in range(slots):
        prod_ref[s] = dot(dpre_ref[col_ref[s]], w_ref[s], ((1,), (1,)))
    for s in range(slots):
        gx_ref[out_idx_ref[s]] += prod_ref[s]
    copies = []
    size = gx_ref.shape[0] // PIECES
    for p in range(PIECES):
        part = pl.ds(p * size, size)
        x_out_ref[part] = gx_ref[part].astype(BF16)
        copies.append(pltpu.make_async_copy(x_out_ref.at[part], gx_out_ref.at[part], sems.at[p]))
        copies[-1].start()
    for copy in copies:
        copy.wait()


def near_kernel(keep_ref, a_ref, b_ref, c_ref, d_ref, stay_ref, up_ref, down_ref):
    for i, out in enumerate((stay_ref, up_ref, down_ref)):
        part = keep_ref[i].astype(F32) + a_ref[i].astype(F32) + b_ref[i].astype(F32)
        out[:SPLIT] = (part[:SPLIT] + c_ref[i].astype(F32)).astype(BF16)
        out[SPLIT:] = (part[SPLIT:] + d_ref[i].astype(F32)).astype(BF16)


def far_kernel(stay_ref, a_ref, b_ref, out_ref):
    out_ref[...] = (stay_ref[...].astype(F32) + a_ref[...].astype(F32) + b_ref[...].astype(F32)).astype(BF16)


def sum_kernel(after_ref, in_ref, out_ref, token_ref):
    out_ref[...] = jnp.sum(in_ref[...].astype(F32), axis=0)
    token_ref[...] = jnp.zeros_like(token_ref)


def write_chunks(own, groups, out_ref, wide_ref, sems):
    rows = out_ref.shape[0]
    for g, (step, part_ref) in enumerate(groups):
        for b in range(4):
            wide_ref[4 * g + b] = part_ref[b].astype(F32)
    for value in range(3):

        @pl.when(own == value)
        def write():
            copies = []
            for g, (step, part_ref) in enumerate(groups):
                for b in range(4):
                    at = (3 * b + (value + step) % 3) * CHUNK
                    size = min(CHUNK, rows - at)
                    copies.append(
                        pltpu.make_async_copy(
                            wide_ref.at[4 * g + b, pl.ds(0, size)],
                            out_ref.at[pl.ds(at, size)],
                            sems.at[4 * g + b],
                        )
                    )
                    copies[-1].start()
            for copy in copies:
                copy.wait()


def own_kernel(own_ref, token_ref, mid_ref, out_ref, wide_ref, sems):
    write_chunks(own_ref[0], [(0, mid_ref)], out_ref, wide_ref, sems)


def rest_kernel(own_ref, done_ref, low_ref, high_ref, out_ref, wide_ref, sems):
    write_chunks(own_ref[0], [(2, low_ref), (1, high_ref)], out_ref, wide_ref, sems)


def first_spread_kernel(in_ref, out_ref):
    value = in_ref[...].astype(BF16)
    for i in range(out_ref.shape[0]):
        out_ref[i] = value


def second_spread_kernel(in_ref, out_ref, sems):
    copies = [
        pltpu.make_async_copy(in_ref, out_ref.at[i], sems.at[i]) for i in range(out_ref.shape[0])
    ]
    for copy in copies:
        copy.start()
    for copy in copies:
        copy.wait()


SMEM = pl.BlockSpec(memory_space=pltpu.SMEM)
VMEM = pl.BlockSpec(memory_space=pltpu.VMEM)
HBM = pl.BlockSpec(memory_space=pltpu.HBM)
ORDER = pl.BlockSpec(memory_space=pl.ANY)


def call(kernel, specs, ins, outs, scratch=(), out_specs=None, aliases=None):
    return pl.pallas_call(
        kernel,
        out_shape=outs,
        in_specs=specs,
        out_specs=out_specs or jax.tree.map(lambda _: VMEM, outs),
        scratch_shapes=scratch,
        input_output_aliases=aliases or {},
        compiler_params=pltpu.CompilerParams(vmem_limit_bytes=40 << 20),
    )(*ins)


def array(shape, kind=BF16):
    return jax.ShapeDtypeStruct(shape, kind)


def run_blocks(idx, out_idx, col, live, rel, own, sib, wb, grad_act):
    slots = wb.shape[0]
    tokens, hidden = grad_act.shape
    cols = hidden // BS
    full, half = array((3, CHUNK, BS)), array((3, SPLIT, BS))
    return call(
        block_kernel,
        [SMEM] * 5 + [VMEM] * 4,
        (idx, out_idx, col, live, rel, own, sib, wb, grad_act),
        (array((tokens, hidden), F32), pltpu.HBM((2 * HALF, tokens, BS), BF16), full, full, full, half, half),
        [
            pltpu.VMEM((2 * HALF, tokens, BS), BF16),
            pltpu.VMEM((slots, tokens, BS), F32),
            pltpu.VMEM((cols, tokens, BS), F32),
            pltpu.VMEM((cols, tokens, BS), BF16),
            pltpu.VMEM((2 * HALF, tokens, BS), F32),
            pltpu.VMEM((NZ, CHUNK, BS), BF16),
            pltpu.VMEM((2 * HALF, tokens, BS), BF16),
            pltpu.SemaphoreType.DMA((PIECES,)),
        ],
        (VMEM, HBM) + (VMEM,) * 5,
    )


def swap(x, axis, groups):
    return lax.all_to_all(x, axis, 0, 0, tiled=True, axis_index_groups=groups)


def shift(x, by):
    return lax.ppermute(x, "dp", [(i, (i + by) % NZ) for i in range(NZ)])


def reduce_gradients(gx, keep, up1, down1, up2, down2, slots):
    tokens = gx.shape[1]
    one = array((CHUNK, BS))
    gx = swap(gx, "mp", None)
    parts = shift(up1, 1), shift(down1, -1), shift(up2, 2), shift(down2, -2)
    stay, up, down = call(near_kernel, [VMEM] * 5, (keep, *parts), (one,) * 3)
    mine = call(far_kernel, [VMEM] * 3, (stay, shift(up, 4), shift(down, -4)), one)

    mid = lax.all_gather(mine, "dp", axis_index_groups=Z_FAR)
    grad_x, token = call(
        sum_kernel, [ORDER, VMEM], (mid, gx), (array((tokens, BS), F32), array((8, BS), F32))
    )
    low, high = shift(mid, 1), shift(mid, -1)
    own = (lax.axis_index("dp") % 3).astype(jnp.int32).reshape(1)
    result = pltpu.HBM((slots * BS, BS), F32)
    grad_w = call(
        own_kernel,
        [SMEM, VMEM, VMEM],
        (own, token, mid),
        result,
        [pltpu.VMEM((4, CHUNK, BS), F32), pltpu.SemaphoreType.DMA((4,))],
        HBM,
    )
    grad_w = call(
        rest_kernel,
        [SMEM, HBM, VMEM, VMEM],
        (own, grad_w, low, high),
        result,
        [pltpu.VMEM((8, CHUNK, BS), F32), pltpu.SemaphoreType.DMA((8,))],
        HBM,
        {1: 0},
    )
    return grad_x, grad_w.reshape(slots, BS, BS)


def local(inputs, block_weights, block_list, grad_act):
    tokens = inputs.shape[0]
    slots = block_weights.shape[0]
    row_ids, col_ids = block_list[:, 0], block_list[:, 1]
    live = (row_ids >= 0).astype(F32)
    row = jnp.maximum(row_ids, 0)
    col = jnp.maximum(col_ids, 0)
    core = lax.axis_index("mp") % NC
    at_y, at_x, at_core = row // (NC * NX), (row // NC) % NX, row % NC
    idx = ((at_core ^ core) * NX + at_x) * NY + at_y
    wb = (block_weights * live[:, None, None]).astype(BF16)

    by_y = call(first_spread_kernel, [VMEM], (inputs,), array((NY, tokens, BS)))
    by_y = swap(by_y, "mp", Y_GROUPS)
    by_xy = call(
        second_spread_kernel,
        [VMEM],
        (by_y,),
        pltpu.HBM((NX, NY, tokens, BS), BF16),
        [pltpu.SemaphoreType.DMA((NX,))],
        HBM,
    )
    by_xy = swap(by_xy, "mp", X_GROUPS)
    own = by_xy.reshape(HALF, tokens, BS)
    sib = lax.ppermute(own, "mp", CORE_SWAP)

    rel = (jnp.arange(NZ, dtype=jnp.int32) + NZ - lax.axis_index("dp")) % NZ
    act, gx, *parts = run_blocks(idx, row, col, live, rel, own, sib, wb, grad_act)
    grad_x, grad_w = reduce_gradients(gx, *parts, slots)
    return act, grad_x, grad_w


def solution(mesh):
    in_specs = (P("dp", "mp"), P("mp", None, None), P("mp", None), P("dp", "mp"))
    out_specs = (P("dp", "mp"), P("dp", "mp"), P("mp", None, None))
    return jax.shard_map(local, mesh=mesh, in_specs=in_specs, out_specs=out_specs, check_vma=False)
```

```python
import jax
import jax.numpy as jnp
from jax import lax
from jax.experimental import pallas as pl
from jax.experimental.pallas import tpu as pltpu
from jax.sharding import PartitionSpec as P

BS = 128
NY, NX, NC = 8, 4, 2
NZ = 12
HALF = NY * NX
Y_GROUPS = [[(y * NX + x) * NC + c for y in range(NY)] for x in range(NX) for c in range(NC)]
X_GROUPS = [[(y * NX + x) * NC + c for x in range(NX)] for y in range(NY) for c in range(NC)]
CORE_SWAP = [(i, i ^ 1) for i in range(HALF * NC)]
CHUNK = 416
SPLIT = 208
PIECES = 8
Z_FAR = [[3 * i + r for i in range(4)] for r in range(3)]
F32, BF16 = jnp.float32, jnp.bfloat16


def gelu_parts(pre):
    inner = 0.7978845608 * (pre + 0.044715 * pre * pre * pre)
    tanh_val = jnp.tanh(inner)
    value = 0.5 * pre * (1.0 + tanh_val)
    slope = 0.5 * (1.0 + tanh_val) + 0.5 * pre * (1.0 - tanh_val * tanh_val) * 0.7978845608 * (
        1.0 + 3.0 * 0.044715 * pre * pre
    )
    return value, slope


def dot(a, b, dims):
    return lax.dot_general(a, b, (dims, ((), ())), preferred_element_type=F32)


def block_kernel(idx_ref, out_idx_ref, col_ref, live_ref, rel_ref, own_ref, sib_ref, w_ref, g_ref,
                 act_ref, gx_out_ref, keep_ref, up1_ref, down1_ref, up2_ref, down2_ref,
                 x_ref, prod_ref, pre_ref, dpre_ref, gx_ref, gw_ref, x_out_ref, act_v_ref, sems):
    slots = w_ref.shape[0]
    col_blocks = pre_ref.shape[0]
    x_ref[:HALF] = own_ref[...]
    x_ref[HALF:] = sib_ref[...]
    pre_ref[...] = jnp.zeros_like(pre_ref)
    for s in range(slots):
        prod_ref[s] = dot(x_ref[idx_ref[s]], w_ref[s], ((1,), (0,)))
    for s in range(slots):
        pre_ref[col_ref[s]] += prod_ref[s]
    for c in range(col_blocks):
        value, slope = gelu_parts(pre_ref[c])
        lanes = slice(c * BS, (c + 1) * BS)
        act_v_ref[:, lanes] = value
        dpre_ref[c] = (g_ref[:, lanes] * slope).astype(BF16)
    act_copy = pltpu.make_async_copy(act_v_ref, act_ref, sems.at[PIECES])
    act_copy.start()
    for s in range(slots):
        wgrad = dot(x_ref[idx_ref[s]], dpre_ref[col_ref[s]], ((0,), (0,)))
        wgrad = (wgrad * live_ref[s]).astype(BF16)
        done = 0
        while done < BS:
            chunk, at = divmod(s * BS + done, CHUNK)
            size = min(BS - done, CHUNK - at)
            gw_ref[rel_ref[chunk], at:at + size] = wgrad[done:done + size]
            done += size
    chunk, at = divmod(slots * BS, CHUNK)
    gw_ref[rel_ref[chunk], at:] = jnp.zeros((CHUNK - at, BS), BF16)
    for i in range(3):
        keep_ref[i] = gw_ref[4 * i]
        up1_ref[i] = gw_ref[4 * i + 1]
        down1_ref[i] = gw_ref[(4 * i + 11) % NZ]
        up2_ref[i] = gw_ref[4 * i + 2, :SPLIT]
        down2_ref[i] = gw_ref[(4 * i + 10) % NZ, SPLIT:]
    gx_ref[...] = jnp.zeros_like(gx_ref)
    for s in range(slots):
        prod_ref[s] = dot(dpre_ref[col_ref[s]], w_ref[s], ((1,), (1,)))
    for s in range(slots):
        gx_ref[out_idx_ref[s]] += prod_ref[s]
    copies = [act_copy]
    size = gx_ref.shape[0] // PIECES
    for p in range(PIECES):
        part = pl.ds(p * size, size)
        x_out_ref[part] = gx_ref[part].astype(BF16)
        copies.append(pltpu.make_async_copy(x_out_ref.at[part], gx_out_ref.at[part], sems.at[p]))
        copies[-1].start()
    for copy in copies:
        copy.wait()


def near_kernel(keep_ref, a_ref, b_ref, c_ref, d_ref, stay_ref, up_ref, down_ref):
    for i, out in enumerate((stay_ref, up_ref, down_ref)):
        part = keep_ref[i].astype(F32) + a_ref[i].astype(F32) + b_ref[i].astype(F32)
        out[:SPLIT] = (part[:SPLIT] + c_ref[i].astype(F32)).astype(BF16)
        out[SPLIT:] = (part[SPLIT:] + d_ref[i].astype(F32)).astype(BF16)


def far_kernel(stay_ref, a_ref, b_ref, out_ref):
    out_ref[...] = (stay_ref[...].astype(F32) + a_ref[...].astype(F32) + b_ref[...].astype(F32)).astype(BF16)


def sum_kernel(after_ref, in_ref, out_ref, token_ref):
    out_ref[...] = jnp.sum(in_ref[...].astype(F32), axis=0)
    token_ref[...] = jnp.zeros_like(token_ref)


def write_chunks(own, groups, out_ref, wide_ref, sems):
    rows = out_ref.shape[0]
    for g, (step, part_ref) in enumerate(groups):
        for b in range(4):
            wide_ref[4 * g + b] = part_ref[b].astype(F32)
    for value in range(3):

        @pl.when(own == value)
        def write():
            copies = []
            for g, (step, part_ref) in enumerate(groups):
                for b in range(4):
                    at = (3 * b + (value + step) % 3) * CHUNK
                    size = min(CHUNK, rows - at)
                    copies.append(
                        pltpu.make_async_copy(
                            wide_ref.at[4 * g + b, pl.ds(0, size)],
                            out_ref.at[pl.ds(at, size)],
                            sems.at[4 * g + b],
                        )
                    )
                    copies[-1].start()
            for copy in copies:
                copy.wait()


def own_kernel(own_ref, token_ref, mid_ref, out_ref, wide_ref, sems):
    write_chunks(own_ref[0], [(0, mid_ref)], out_ref, wide_ref, sems)


def rest_kernel(own_ref, done_ref, low_ref, high_ref, out_ref, wide_ref, sems):
    write_chunks(own_ref[0], [(2, low_ref), (1, high_ref)], out_ref, wide_ref, sems)


def first_spread_kernel(in_ref, out_ref):
    value = in_ref[...].astype(BF16)
    for i in range(out_ref.shape[0]):
        out_ref[i] = value


def second_spread_kernel(in_ref, out_ref, sems):
    copies = [
        pltpu.make_async_copy(in_ref, out_ref.at[i], sems.at[i]) for i in range(out_ref.shape[0])
    ]
    for copy in copies:
        copy.start()
    for copy in copies:
        copy.wait()


SMEM = pl.BlockSpec(memory_space=pltpu.SMEM)
VMEM = pl.BlockSpec(memory_space=pltpu.VMEM)
HBM = pl.BlockSpec(memory_space=pltpu.HBM)
ORDER = pl.BlockSpec(memory_space=pl.ANY)


def call(kernel, specs, ins, outs, scratch=(), out_specs=None, aliases=None):
    return pl.pallas_call(
        kernel,
        out_shape=outs,
        in_specs=specs,
        out_specs=out_specs or jax.tree.map(lambda _: VMEM, outs),
        scratch_shapes=scratch,
        input_output_aliases=aliases or {},
        compiler_params=pltpu.CompilerParams(vmem_limit_bytes=40 << 20),
    )(*ins)


def array(shape, kind=BF16):
    return jax.ShapeDtypeStruct(shape, kind)


def run_blocks(idx, out_idx, col, live, rel, own, sib, wb, grad_act):
    slots = wb.shape[0]
    tokens, hidden = grad_act.shape
    cols = hidden // BS
    full, half = array((3, CHUNK, BS)), array((3, SPLIT, BS))
    return call(
        block_kernel,
        [SMEM] * 5 + [VMEM] * 4,
        (idx, out_idx, col, live, rel, own, sib, wb, grad_act),
        (pltpu.HBM((tokens, hidden), F32), pltpu.HBM((2 * HALF, tokens, BS), BF16), full, full, full, half, half),
        [
            pltpu.VMEM((2 * HALF, tokens, BS), BF16),
            pltpu.VMEM((slots, tokens, BS), F32),
            pltpu.VMEM((cols, tokens, BS), F32),
            pltpu.VMEM((cols, tokens, BS), BF16),
            pltpu.VMEM((2 * HALF, tokens, BS), F32),
            pltpu.VMEM((NZ, CHUNK, BS), BF16),
            pltpu.VMEM((2 * HALF, tokens, BS), BF16),
            pltpu.VMEM((tokens, hidden), F32),
            pltpu.SemaphoreType.DMA((PIECES + 1,)),
        ],
        (HBM, HBM) + (VMEM,) * 5,
    )


def swap(x, axis, groups):
    return lax.all_to_all(x, axis, 0, 0, tiled=True, axis_index_groups=groups)


def shift(x, by):
    return lax.ppermute(x, "dp", [(i, (i + by) % NZ) for i in range(NZ)])


def reduce_gradients(gx, keep, up1, down1, up2, down2, slots):
    tokens = gx.shape[1]
    one = array((CHUNK, BS))
    gx = swap(gx, "mp", None)
    parts = shift(up1, 1), shift(down1, -1), shift(up2, 2), shift(down2, -2)
    stay, up, down = call(near_kernel, [VMEM] * 5, (keep, *parts), (one,) * 3)
    mine = call(far_kernel, [VMEM] * 3, (stay, shift(up, 4), shift(down, -4)), one)

    mid = lax.all_gather(mine, "dp", axis_index_groups=Z_FAR)
    grad_x, token = call(
        sum_kernel, [ORDER, VMEM], (mid, gx), (array((tokens, BS), F32), array((8, BS), F32))
    )
    low, high = shift(mid, 1), shift(mid, -1)
    own = (lax.axis_index("dp") % 3).astype(jnp.int32).reshape(1)
    result = pltpu.HBM((slots * BS, BS), F32)
    grad_w = call(
        own_kernel,
        [SMEM, VMEM, VMEM],
        (own, token, mid),
        result,
        [pltpu.VMEM((4, CHUNK, BS), F32), pltpu.SemaphoreType.DMA((4,))],
        HBM,
    )
    grad_w = call(
        rest_kernel,
        [SMEM, HBM, VMEM, VMEM],
        (own, grad_w, low, high),
        result,
        [pltpu.VMEM((8, CHUNK, BS), F32), pltpu.SemaphoreType.DMA((8,))],
        HBM,
        {1: 0},
    )
    return grad_x, grad_w.reshape(slots, BS, BS)


def local(inputs, block_weights, block_list, grad_act):
    tokens = inputs.shape[0]
    slots = block_weights.shape[0]
    row_ids, col_ids = block_list[:, 0], block_list[:, 1]
    live = (row_ids >= 0).astype(F32)
    row = jnp.maximum(row_ids, 0)
    col = jnp.maximum(col_ids, 0)
    core = lax.axis_index("mp") % NC
    at_y, at_x, at_core = row // (NC * NX), (row // NC) % NX, row % NC
    idx = ((at_core ^ core) * NX + at_x) * NY + at_y
    wb = (block_weights * live[:, None, None]).astype(BF16)

    by_y = call(first_spread_kernel, [VMEM], (inputs,), array((NY, tokens, BS)))
    by_y = swap(by_y, "mp", Y_GROUPS)
    by_xy = call(
        second_spread_kernel,
        [VMEM],
        (by_y,),
        pltpu.HBM((NX, NY, tokens, BS), BF16),
        [pltpu.SemaphoreType.DMA((NX,))],
        HBM,
    )
    by_xy = swap(by_xy, "mp", X_GROUPS)
    own = by_xy.reshape(HALF, tokens, BS)
    sib = lax.ppermute(own, "mp", CORE_SWAP)

    rel = (jnp.arange(NZ, dtype=jnp.int32) + NZ - lax.axis_index("dp")) % NZ
    act, gx, *parts = run_blocks(idx, row, col, live, rel, own, sib, wb, grad_act)
    grad_x, grad_w = reduce_gradients(gx, *parts, slots)
    return act, grad_x, grad_w


def solution(mesh):
    in_specs = (P("dp", "mp"), P("mp", None, None), P("mp", None), P("dp", "mp"))
    out_specs = (P("dp", "mp"), P("dp", "mp"), P("mp", None, None))
    return jax.shard_map(local, mesh=mesh, in_specs=in_specs, out_specs=out_specs, check_vma=False)
```
